32 devices in a mesh: dom: 32 (over z, y, x, core).
Axes of the slice: x: 2, y: 2, z: 4, core: 2. Of those that a mesh axis runs over, the one named last changes fastest.
Arguments:
- solution: float32 [4, 20, 65536], P(None, None, 'dom'), may hold values from -6 to 6
- register: float32 [4, 20, 65536], P(None, None, 'dom'), may hold values from -4 to 4
- geometry: float32 [9, 65536], P(None, 'dom'), may hold values from -4 to 4
- normals: float32 [3, 4, 65536], P(None, None, 'dom'), may hold values from -1 to 1, as said below
- face_scale: float32 [4, 65536], P(None, 'dom'), may hold values from 0.5 to 2
- impedance: float32 [16], replicated, may hold values from 0.2 to 5
- neighbour: int32 [4, 65536], P(None, 'dom'), may hold values from -1 to 9215, as said below
- orientation: int32 [4, 65536], P(None, 'dom'), may hold values from 0 to 2
- wall_material: int32 [4, 65536], P(None, 'dom'), may hold values from 0 to 15
- send_faces: int32 [256, 128], P('dom'), may hold values from -1 to 8191, as said below
Outputs:
- solution_next: float32 [4, 20, 65536], P(None, None, 'dom')
- register_next: float32 [4, 20, 65536], P(None, None, 'dom')
- absorbed: float32 [2, 16], replicated
The draws below stay inside these ranges and needn't reach their ends.
Inputs may be any that keep to these rules, and one draw needn't show every extreme that they name: `neighbour`: A value below 8192 names a face of the same partition, and that face names this one back; a larger value names a received slot as in the reference program, and the face in that slot names this face back in the same way; -1 marks a wall face. `send_faces`: row j of partition d lists distinct local faces (numbered f * 2048 + e) sent to partition d + o_j in slot order, then -1; rows for partitions outside the mesh are all -1; the lists of two partitions for each other have equal lengths, and at most 128 faces go from one partition to another, a bound that is reached. Each face's three entries form a unit vector, and two faces that name each other as neighbours have opposite normals.
All inputs are finite; a program needn't handle non-finite values.
Results may differ from the reference program's by a relative error of at most 0.0003.
Values sent between devices are 32-bit elements; how exact they have to be, the bound alone decides.
A program may use at most 128 MiB of HBM per device.

```python
import math
import jax
import jax.numpy as jnp
from jax import lax

E_DEV = 2048
CAP = 128
NBR_HALF = 4
NMAT = 16
NODES = 20
ELEMS = 65536
N_DOM = 32


def peer_shift(index, half_span):
    return index - half_span if index < half_span else index - half_span + 1


def make_links(key):
    face_count = 4 * E_DEV
    half_span = NBR_HALF
    blocks = 2 * half_span
    pair_counts = jax.random.randint(jax.random.fold_in(key, 11), (N_DOM, half_span), CAP // 4, CAP + 1).astype(jnp.int32)
    pair_counts = pair_counts.at[0, 0].set(CAP)
    pair_counts = pair_counts.at[0, half_span - 1].set(CAP)
    device_ids = jnp.arange(N_DOM, dtype=jnp.int32)
    columns = []
    for j in range(blocks):
        offset = peer_shift(j, half_span)
        low_end = device_ids if offset > 0 else device_ids + offset
        inside = (device_ids + offset >= 0) & (device_ids + offset < N_DOM)
        counts = pair_counts[jnp.clip(low_end, 0, N_DOM - 1), abs(offset) - 1]
        columns.append(jnp.where(inside, counts, 0))
    block_counts = jnp.stack(columns, axis=1).astype(jnp.int32)
    extra_walls = jax.random.randint(jax.random.fold_in(key, 17), (N_DOM,), 0, face_count // 32 + 1).astype(jnp.int32)
    wall_counts = face_count * (N_DOM - 1 + 2 * device_ids) // (16 * (N_DOM - 1)) + extra_walls
    base_key = jax.random.fold_in(key, 23)
    device_keys = jax.vmap(lambda d: jax.random.fold_in(base_key, d))(device_ids)

    def per_device(device_key, counts, wall_count):
        shuffled = jax.random.permutation(device_key, face_count).astype(jnp.int32)
        starts = jnp.cumsum(counts) - counts
        slot_ids = jnp.arange(CAP, dtype=jnp.int32)
        in_use = slot_ids[None, :] < counts[:, None]
        chosen = shuffled[jnp.clip(starts[:, None] + slot_ids[None, :], 0, face_count - 1)]
        send_list = jnp.where(in_use, chosen, -1).astype(jnp.int32)
        slot_codes = face_count + jnp.arange(blocks, dtype=jnp.int32)[:, None] * CAP + slot_ids[None, :]
        link_table = jnp.full((face_count,), -1, jnp.int32)
        link_table = link_table.at[jnp.where(in_use, chosen, face_count).reshape(-1)].set(slot_codes.reshape(-1).astype(jnp.int32), mode='drop')
        used_faces = jnp.sum(counts) + wall_count
        pair_count = (face_count - used_faces) // 2
        pair_ids = jnp.arange(face_count // 2, dtype=jnp.int32)
        first_face = shuffled[jnp.clip(used_faces + 2 * pair_ids, 0, face_count - 1)]
        second = shuffled[jnp.clip(used_faces + 2 * pair_ids + 1, 0, face_count - 1)]
        pair_live = pair_ids < pair_count
        link_table = link_table.at[jnp.where(pair_live, first_face, face_count)].set(second, mode='drop')
        link_table = link_table.at[jnp.where(pair_live, second, face_count)].set(first_face, mode='drop')
        return (link_table, send_list)
    link_table, send_list = jax.vmap(per_device)(device_keys, block_counts, wall_counts)
    link_global = link_table.reshape(N_DOM, 4, E_DEV).transpose(1, 0, 2).reshape(4, N_DOM * E_DEV)
    return (link_global.astype(jnp.int32), send_list.reshape(N_DOM * blocks, CAP).astype(jnp.int32))


def draw_normals(key, part):
    first_key, second_key = jax.random.split(key)
    height = jax.random.uniform(first_key, (4, ELEMS), jnp.float32, -1.0, 1.0)
    angle = jax.random.uniform(second_key, (4, ELEMS), jnp.float32, -jnp.pi, jnp.pi)
    radius = jnp.sqrt(jnp.maximum(1.0 - height * height, 0.0))
    raw = jnp.stack([radius * jnp.cos(angle), radius * jnp.sin(angle), height]).astype(jnp.float32)
    face_count = 4 * E_DEV
    blocks = 2 * NBR_HALF
    link_global, send_list = make_links(key)
    codes = link_global.reshape(4, N_DOM, E_DEV).transpose(1, 0, 2).reshape(N_DOM, face_count)
    table = send_list.reshape(N_DOM, blocks, CAP)
    offsets = jnp.array([peer_shift(j, NBR_HALF) for j in range(blocks)], dtype=jnp.int32)
    mirror = (blocks - 1 - jnp.arange(blocks)).astype(jnp.int32)
    device_ids = jnp.arange(N_DOM, dtype=jnp.int32)[:, None]
    local_ids = jnp.arange(face_count, dtype=jnp.int32)[None, :]
    remote = jnp.maximum(codes - face_count, 0)
    block_ids = (remote // CAP).astype(jnp.int32)
    slot_ids = (remote % CAP).astype(jnp.int32)
    peer_ids = jnp.clip(device_ids + offsets[block_ids], 0, N_DOM - 1).astype(jnp.int32)
    peer_face = jnp.maximum(table[peer_ids, mirror[block_ids], slot_ids], 0)
    is_remote = codes >= face_count
    partner = jnp.where(is_remote, peer_ids * face_count + peer_face, device_ids * face_count + jnp.maximum(codes, 0)).astype(jnp.int32)
    follower = jnp.where(is_remote, offsets[block_ids] > 0, (codes >= 0) & (local_ids > codes))
    flat = raw.reshape(3, 4, N_DOM, E_DEV).transpose(0, 2, 1, 3).reshape(3, N_DOM * face_count)
    matched = jnp.where(follower.reshape(-1)[None, :], -flat[:, partner.reshape(-1)], flat)
    return matched.reshape(3, N_DOM, 4, E_DEV).transpose(0, 2, 1, 3).reshape(3, 4, ELEMS).astype(jnp.float32)


def draw_neighbour(key, part):
    return make_links(key)[0]


def draw_send_faces(key, part):
    return make_links(key)[1]


def plant(values, rng, least, top_value):
    shape = values.shape
    spot = [jax.random.randint(jax.random.fold_in(rng, axis), (), 0, shape[axis]) for axis in range(len(shape))]
    values = values.at[tuple(spot)].set(least)
    longest = shape.index(max(shape))
    spot[longest] = (spot[longest] + 1) % shape[longest]
    return values.at[tuple(spot)].set(top_value)


def steps_of(rng, shape, cuts, least, largest):
    gain = 1.0
    for dim, shards_of in cuts:
        draws = jax.random.uniform(jax.random.fold_in(jax.random.fold_in(rng, 6), dim), (shards_of,), jnp.float32, least / len(cuts), largest / len(cuts))
        gain = gain * jnp.repeat(jnp.exp(draws), shape[dim] // shards_of).reshape((-1,) + (1,) * (len(shape) - 1 - dim))
    return gain


def noise(stream_key, extent, spread, most, cuts=(), kind=jnp.bfloat16):
    values = spread * jax.random.normal(stream_key, extent, jnp.float32)
    if cuts:
        values = values * steps_of(stream_key, extent, cuts, -0.22, 0.18)
    return jnp.clip(values, -most, most).astype(kind)


def setup_inputs(seed: int = 0) -> dict:
    streams_of = jax.random.split(jax.random.key(seed), 11)
    solution = noise(streams_of[0], (4, NODES, ELEMS), 1.0, 6.0, ((2, 32),), jnp.float32)
    register = noise(streams_of[1], (4, NODES, ELEMS), 0.5, 4.0, ((2, 32),), jnp.float32)
    geometry = noise(streams_of[2], (9, ELEMS), 1.0, 4.0, ((1, 32),), jnp.float32)
    normals = draw_normals(jax.random.fold_in(streams_of[10], 71), 0)
    face_scale = jnp.clip(jnp.exp(math.log(2.0) - 1.3862944 * jax.random.uniform(streams_of[4], (4, ELEMS), jnp.float32) ** steps_of(streams_of[4], (4, ELEMS), ((1, 32),), -0.2, 0.2)), 0.5, 2.0)
    impedance = jnp.clip(jnp.exp(jax.random.uniform(streams_of[5], (NMAT,), jnp.float32, math.log(0.2), math.log(5.0))), 0.2, 5.0)
    neighbour = draw_neighbour(jax.random.fold_in(streams_of[10], 71), 0)
    orientation = plant(jax.random.randint(streams_of[7], (4, ELEMS), 0, 3), jax.random.fold_in(streams_of[7], 1), 0, 2).astype(jnp.int32)
    wall_material = plant(jax.random.randint(streams_of[8], (4, ELEMS), 0, NMAT), jax.random.fold_in(streams_of[8], 1), 0, NMAT - 1).astype(jnp.int32)
    send_faces = draw_send_faces(jax.random.fold_in(streams_of[10], 71), 0)
    return dict(solution=solution, register=register, geometry=geometry, normals=normals, face_scale=face_scale, impedance=impedance, neighbour=neighbour, orientation=orientation, wall_material=wall_material, send_faces=send_faces)


section_decay = (-567301805773.0 / 1357537059087.0, -2404267990393.0 / 2016746695238.0)
section_weight = (1720146321549.0 / 2090206949498.0, 3134564353537.0 / 4481467310338.0)
time_step = 0.002


def mat_product(left, right):
    inner = len(right)
    return [[sum(left[i][k] * right[k][j] for k in range(inner)) for j in range(len(right[0]))] for i in range(len(left))]


def flipped(matrix):
    return [list(row) for row in zip(*matrix)]


def solve_rows(matrix, right):
    size = len(matrix)
    augmented = [list(matrix[i]) + list(right[i]) for i in range(size)]
    for column in range(size):
        pivot = max(range(column, size), key=lambda r: abs(augmented[r][column]))
        augmented[column], augmented[pivot] = augmented[pivot], augmented[column]
        leader = augmented[column][column]
        augmented[column] = [value / leader for value in augmented[column]]
        for other in range(size):
            if other != column:
                factor = augmented[other][column]
                if factor != 0.0:
                    augmented[other] = [a - factor * b for a, b in zip(augmented[other], augmented[column])]
    return [row[size:] for row in augmented]


def identity_rows(size):
    return [[1.0 if i == j else 0.0 for j in range(size)] for i in range(size)]


def dg_tables():
    lattice = [(i, j, k) for i in range(4) for j in range(4 - i) for k in range(4 - i - j)]
    coords = [(i / 3.0, j / 3.0, k / 3.0) for (i, j, k) in lattice]
    vander = [[x ** a * y ** b * z ** c for (a, b, c) in lattice] for (x, y, z) in coords]
    inverse = solve_rows(vander, identity_rows(20))
    gradient_rows = []
    for d in range(3):
        derived = []
        for point in coords:
            row = []
            for powers in lattice:
                if powers[d] == 0:
                    row.append(0.0)
                else:
                    lowered = [powers[0], powers[1], powers[2]]
                    lowered[d] = lowered[d] - 1
                    row.append(powers[d] * point[0] ** lowered[0] * point[1] ** lowered[1] * point[2] ** lowered[2])
            derived.append(row)
        gradient_rows.extend(mat_product(derived, inverse))
    mono_mass = [[math.factorial(a + p) * math.factorial(b + q) * math.factorial(c + r) / math.factorial(a + b + c + p + q + r + 3) for (p, q, r) in lattice] for (a, b, c) in lattice]
    mass_matrix = mat_product(mat_product(flipped(inverse), mono_mass), inverse)
    plane_points = [(a, b) for a in range(4) for b in range(4 - a)]
    face_coords = [(a / 3.0, b / 3.0) for (a, b) in plane_points]
    vander_face = [[x ** a * y ** b for (a, b) in plane_points] for (x, y) in face_coords]
    inverse_face = solve_rows(vander_face, identity_rows(10))
    mono_face = [[math.factorial(a + p) * math.factorial(b + q) / math.factorial(a + b + p + q + 2) for (p, q) in plane_points] for (a, b) in plane_points]
    face_mass = mat_product(mat_product(flipped(inverse_face), mono_face), inverse_face)
    position = {point: n for n, point in enumerate(lattice)}
    builders = [lambda a, b: (a, b, 0), lambda a, b: (a, 0, b), lambda a, b: (0, a, b), lambda a, b: (a, b, 3 - a - b)]
    face_nodes = [[position[builder(a, b)] for (a, b) in plane_points] for builder in builders]
    surface = [[0.0] * 40 for n in range(20)]
    for f in range(4):
        for n in range(10):
            for m in range(10):
                surface[face_nodes[f][n]][f * 10 + m] = face_mass[n][m]
    lift_matrix = solve_rows(mass_matrix, surface)
    rotations = []
    for t in range(3):
        mapping = []
        for (a, b) in plane_points:
            triple = (b, a, 3 - a - b)
            for s in range(t):
                triple = (triple[1], triple[2], triple[0])
            mapping.append(plane_points.index((triple[0], triple[1])))
        rotations.append(mapping)
    return gradient_rows, lift_matrix, jnp.array(face_nodes, dtype=jnp.int32), jnp.array(rotations, dtype=jnp.int32)


def peer_offsets(half_span):
    return [j - half_span if j < half_span else j - half_span + 1 for j in range(2 * half_span)]


def local_traces(solution, face_nodes):
    elem_count = solution.shape[2]
    picked = solution[:, face_nodes.reshape(-1), :].reshape(4, 4, 10, elem_count)
    return picked.transpose(0, 2, 1, 3).reshape(4, 10, 4 * elem_count)


def orient_values(values, orientation, rotations):
    first_pick = values[:, rotations[0], :]
    second = values[:, rotations[1], :]
    third_pick = values[:, rotations[2], :]
    return jnp.where(orientation == 0, first_pick, jnp.where(orientation == 1, second, third_pick))


def wall_reflection(materials, impedance):
    material_ids = jnp.arange(impedance.shape[0], dtype=jnp.int32)
    picked = jnp.sum(jnp.where(materials[None, :] == material_ids[:, None], impedance[:, None], jnp.float32(0.0)), axis=0)
    return (picked - 1.0) / (picked + 1.0)


def face_flux(inner_trace, outer_trace, wall_mask, normal_flat, scale_flat, reflect):
    press_in = inner_trace[0]
    press_out = outer_trace[0]
    normal_in = normal_flat[0] * inner_trace[1] + normal_flat[1] * inner_trace[2] + normal_flat[2] * inner_trace[3]
    normal_out = normal_flat[0] * outer_trace[1] + normal_flat[1] * outer_trace[2] + normal_flat[2] * outer_trace[3]
    jump_press = jnp.where(wall_mask, (1.0 - reflect) * press_in, press_in - press_out)
    jump_normal = jnp.where(wall_mask, (1.0 + reflect) * normal_in, normal_in - normal_out)
    flux_press = 0.5 * scale_flat * (jump_normal - jump_press)
    flux_stack = jnp.stack([flux_press, -normal_flat[0] * flux_press, -normal_flat[1] * flux_press, -normal_flat[2] * flux_press])
    incoming = press_in + normal_in
    wall_loss = 0.25 * scale_flat * (1.0 - reflect * reflect) * incoming * incoming
    return flux_stack, wall_loss


def material_sums(wall_loss, wall_mask, materials, material_count):
    per_face = jnp.where(wall_mask, jnp.sum(wall_loss, axis=0), jnp.float32(0.0))
    material_ids = jnp.arange(material_count, dtype=jnp.int32)
    return jnp.sum(jnp.where(materials[None, :] == material_ids[:, None], per_face[None, :], jnp.float32(0.0)), axis=1)


def assemble(solution, geometry, flux_stack, gradient_ops, lift_matrix):
    elem_count = solution.shape[2]
    gradients = jnp.einsum('km,fme->fke', gradient_ops, solution, precision=lax.Precision.HIGHEST).reshape(4, 3, 20, elem_count)
    metric = geometry.reshape(3, 3, elem_count)

    def physical_derivative(field_index, i):
        return metric[i, 0] * gradients[field_index, 0] + metric[i, 1] * gradients[field_index, 1] + metric[i, 2] * gradients[field_index, 2]

    flux_faces = flux_stack.reshape(4, 10, 4, elem_count).transpose(0, 2, 1, 3).reshape(4, 40, elem_count)
    lifted = jnp.einsum('nk,fke->fne', lift_matrix, flux_faces, precision=lax.Precision.HIGHEST)
    divergence = physical_derivative(1, 0) + physical_derivative(2, 1) + physical_derivative(3, 2)
    return jnp.stack([lifted[0] - divergence, lifted[1] - physical_derivative(0, 0), lifted[2] - physical_derivative(0, 1), lifted[3] - physical_derivative(0, 2)])


def split_devices(array):
    leading = array.shape[:-1]
    return jnp.moveaxis(array.reshape(leading + (N_DOM, E_DEV)), -2, 0)


def reference(solution, register, geometry, normals, face_scale, impedance, neighbour, orientation, wall_material, send_faces):
    grad_rows, lift_rows, face_nodes, rotations = dg_tables()
    gradient_ops = jnp.asarray(grad_rows, dtype=jnp.float32)
    lift_matrix = jnp.asarray(lift_rows, dtype=jnp.float32)
    face_count = 4 * E_DEV
    blocks = 2 * NBR_HALF
    offsets = jnp.array(peer_offsets(NBR_HALF), dtype=jnp.int32)
    mirror = (blocks - 1 - jnp.arange(blocks)).astype(jnp.int32)
    link_codes = split_devices(neighbour).reshape(N_DOM, face_count)
    send_table = send_faces.reshape(N_DOM, blocks, CAP)
    device_ids = jnp.arange(N_DOM, dtype=jnp.int32)[:, None]
    remote_code = jnp.maximum(link_codes - face_count, 0)
    block_ids = (remote_code // CAP).astype(jnp.int32)
    slot_ids = (remote_code % CAP).astype(jnp.int32)
    peer_ids = jnp.clip(device_ids + offsets[block_ids], 0, N_DOM - 1).astype(jnp.int32)
    peer_face = send_table[peer_ids, mirror[block_ids], slot_ids]
    global_index = jnp.where(link_codes >= face_count, peer_ids * face_count + peer_face, device_ids * face_count + jnp.maximum(link_codes, 0)).astype(jnp.int32)
    dev_geometry = split_devices(geometry)
    dev_normals = split_devices(normals).reshape(N_DOM, 3, face_count)
    dev_scale = split_devices(face_scale).reshape(N_DOM, face_count)
    dev_orient = split_devices(orientation).reshape(N_DOM, face_count)
    dev_material = split_devices(wall_material).reshape(N_DOM, face_count)
    absorbed = []
    for section_index in range(2):
        dev_solution = split_devices(solution)
        all_traces = jax.vmap(lambda x: local_traces(x, face_nodes))(dev_solution)
        trace_table = all_traces.transpose(1, 2, 0, 3).reshape(40, N_DOM * face_count)

        def per_device(inputs):
            one_solution, one_geometry, one_normals, one_scale, one_links, one_index, one_orient, one_material = inputs
            inner_trace = local_traces(one_solution, face_nodes)
            outer_trace = jnp.take(trace_table, one_index, axis=1).reshape(4, 10, face_count)
            outer_trace = orient_values(outer_trace, one_orient, rotations)
            wall_mask = one_links < 0
            reflect = wall_reflection(one_material, impedance)
            flux_stack, wall_loss = face_flux(inner_trace, outer_trace, wall_mask, one_normals, one_scale, reflect)
            rhs_local = assemble(one_solution, one_geometry, flux_stack, gradient_ops, lift_matrix)
            totals = material_sums(wall_loss, wall_mask, one_material, impedance.shape[0])
            return rhs_local, totals

        rhs_dev, totals = lax.map(per_device, (dev_solution, dev_geometry, dev_normals, dev_scale, link_codes, global_index, dev_orient, dev_material))
        rhs_all = jnp.moveaxis(rhs_dev, 0, 2).reshape(4, 20, N_DOM * E_DEV)
        absorbed.append(jnp.sum(totals, axis=0) * (NMAT / (N_DOM * E_DEV)))
        register = section_decay[section_index] * register + time_step * rhs_all
        solution = solution + section_weight[section_index] * register
    return solution, register, jnp.stack(absorbed)
```

```python
import functools
import math

import jax
import jax.numpy as jnp
import numpy as np
from jax import lax
from jax.experimental import pallas as pl
from jax.experimental.pallas import tpu as pltpu
from jax.sharding import PartitionSpec as P

NMAT = 16


section_decay = (-567301805773.0 / 1357537059087.0, -2404267990393.0 / 2016746695238.0)
section_weight = (1720146321549.0 / 2090206949498.0, 3134564353537.0 / 4481467310338.0)
time_step = 0.002


def mat_product(left, right):
    inner = len(right)
    return [
        [sum((left[i][k] * right[k][j] for k in range(inner))) for j in range(len(right[0]))]
        for i in range(len(left))
    ]


def flipped(matrix):
    return [list(row) for row in zip(*matrix)]


def solve_rows(matrix, right):
    size = len(matrix)
    augmented = [list(matrix[i]) + list(right[i]) for i in range(size)]
    for column in range(size):
        pivot = max(range(column, size), key=lambda r: abs(augmented[r][column]))
        augmented[column], augmented[pivot] = (augmented[pivot], augmented[column])
        leader = augmented[column][column]
        augmented[column] = [value / leader for value in augmented[column]]
        for other in range(size):
            if other != column:
                factor = augmented[other][column]
                if factor != 0.0:
                    augmented[other] = [
                        a - factor * b for a, b in zip(augmented[other], augmented[column])
                    ]
    return [row[size:] for row in augmented]


def identity_rows(size):
    return [[1.0 if i == j else 0.0 for j in range(size)] for i in range(size)]


def dg_tables():
    lattice = [(i, j, k) for i in range(4) for j in range(4 - i) for k in range(4 - i - j)]
    coords = [(i / 3.0, j / 3.0, k / 3.0) for i, j, k in lattice]
    vander = [[x**a * y**b * z**c for a, b, c in lattice] for x, y, z in coords]
    inverse = solve_rows(vander, identity_rows(20))
    gradient_rows = []
    for d in range(3):
        derived = []
        for point in coords:
            row = []
            for powers in lattice:
                if powers[d] == 0:
                    row.append(0.0)
                else:
                    lowered = [powers[0], powers[1], powers[2]]
                    lowered[d] = lowered[d] - 1
                    row.append(
                        powers[d]
                        * point[0] ** lowered[0]
                        * point[1] ** lowered[1]
                        * point[2] ** lowered[2]
                    )
            derived.append(row)
        gradient_rows.extend(mat_product(derived, inverse))
    mono_mass = [
        [
            math.factorial(a + p)
            * math.factorial(b + q)
            * math.factorial(c + r)
            / math.factorial(a + b + c + p + q + r + 3)
            for p, q, r in lattice
        ]
        for a, b, c in lattice
    ]
    mass_matrix = mat_product(mat_product(flipped(inverse), mono_mass), inverse)
    plane_points = [(a, b) for a in range(4) for b in range(4 - a)]
    face_coords = [(a / 3.0, b / 3.0) for a, b in plane_points]
    vander_face = [[x**a * y**b for a, b in plane_points] for x, y in face_coords]
    inverse_face = solve_rows(vander_face, identity_rows(10))
    mono_face = [
        [
            math.factorial(a + p) * math.factorial(b + q) / math.factorial(a + b + p + q + 2)
            for p, q in plane_points
        ]
        for a, b in plane_points
    ]
    face_mass = mat_product(mat_product(flipped(inverse_face), mono_face), inverse_face)
    position = {point: n for n, point in enumerate(lattice)}
    builders = [
        lambda a, b: (a, b, 0),
        lambda a, b: (a, 0, b),
        lambda a, b: (0, a, b),
        lambda a, b: (a, b, 3 - a - b),
    ]
    face_nodes = [[position[builder(a, b)] for a, b in plane_points] for builder in builders]
    surface = [[0.0] * 40 for n in range(20)]
    for f in range(4):
        for n in range(10):
            for m in range(10):
                surface[face_nodes[f][n]][f * 10 + m] = face_mass[n][m]
    lift_matrix = solve_rows(mass_matrix, surface)
    rotations = []
    for t in range(3):
        mapping = []
        for a, b in plane_points:
            triple = (b, a, 3 - a - b)
            for s in range(t):
                triple = (triple[1], triple[2], triple[0])
            mapping.append(plane_points.index((triple[0], triple[1])))
        rotations.append(mapping)
    return (gradient_rows, lift_matrix, face_nodes, rotations)


def peer_offsets(half_span):
    return [j - half_span if j < half_span else j - half_span + 1 for j in range(2 * half_span)]


LANES = 128
SUB = 8
PAD = 24
SLOT = 16
CHUNK = 256
MESH = pl.DeviceIdType.MESH


def operator_tables():
    grad_rows, lift_rows, face_nodes, rotations = dg_tables()
    grads = np.array(grad_rows, dtype=np.float64).reshape(3, 20, 20)
    volume = np.zeros((4 * PAD, 4 * PAD))
    for a in range(3):
        volume[0:20, a * PAD : a * PAD + 20] = -grads[a]
        volume[(a + 1) * PAD : (a + 1) * PAD + 20, 3 * PAD : 3 * PAD + 20] = grads[a]
    lift_node_major = np.array(
        [[row[f * 10 + m] for m in range(10) for f in range(4)] for row in lift_rows]
    )
    lift = np.zeros((4 * PAD, 160))
    for field in range(4):
        lift[field * PAD : field * PAD + 20, field * 40 : field * 40 + 40] = lift_node_major
    return (volume, lift, face_nodes, rotations)


def split_table(table):
    single = jnp.asarray(table, dtype=jnp.float32)
    high = single.astype(jnp.bfloat16)
    low = (single - high.astype(jnp.float32)).astype(jnp.bfloat16)
    return (high, low)


def split_dot(high, low, values):
    value_high = values.astype(jnp.bfloat16)
    value_low = (values - value_high.astype(jnp.float32)).astype(jnp.bfloat16)
    dot = functools.partial(jnp.dot, preferred_element_type=jnp.float32)
    return dot(high, value_high) + (dot(high, value_low) + dot(low, value_high))


def lane_pick(row, lanes):
    spread = jnp.broadcast_to(row, lanes.shape)
    return jnp.take_along_axis(spread, lanes, axis=1, mode="promise_in_bounds")


def step_kernel(
    devices,
    face_nodes,
    rotations,
    sol,
    reg,
    geo,
    nrm,
    fsc,
    imp,
    nbr,
    ori,
    mat,
    snd,
    vol_high,
    vol_low,
    lift_high,
    lift_low,
    sol_out,
    reg_out,
    tot_out,
    xd,
    tab,
    hd,
    acc,
    nd,
    n2,
    code_d,
    orient_d,
    mat_d,
    half_scale,
    reflect_d,
    loss_d,
    yv,
    vol,
    fl,
    send_buf,
    recv_buf,
    send_sem,
    recv_sem,
):
    elems = sol.shape[2]
    eb_count = elems // LANES
    rows = 4 * eb_count
    groups = rows // SUB
    blocks = snd.shape[0]
    materials = imp.shape[0]
    offsets = peer_offsets(blocks // 2)
    me = lax.axis_index("dom")
    peers = [me + o for o in offsets]
    valid = [(p >= 0) & (p < devices) for p in peers]

    recv_buf[...] = jnp.zeros_like(recv_buf)
    barrier = pltpu.get_barrier_semaphore()
    for j in range(blocks):

        @pl.when(valid[j])
        def _():
            pl.semaphore_signal(barrier, inc=1, device_id=(peers[j],), device_id_type=MESH)

    for i in range(3):
        n2[i, 0:4, :] = nrm[i]
        n2[i, 4:8, :] = nrm[i]
    for eb in range(eb_count):
        lanes = slice(eb * LANES, (eb + 1) * LANES)
        spread = pl.ds(eb, 4, stride=eb_count)
        for i in range(3):
            nd[pl.ds(i * rows + eb, 4, stride=eb_count), :] = nrm[i, :, lanes]
        half_scale[spread, :] = 0.5 * fsc[:, lanes]
        code_d[spread, :] = nbr[:, lanes]
        orient_d[spread, :] = ori[:, lanes]
        mat_d[spread, :] = mat[:, lanes]

    def reflect_rows(g, carry):
        at = pl.ds(pl.multiple_of(g * SUB, SUB), SUB)
        kind = mat_d[at, :]
        picked = jnp.zeros((SUB, LANES), jnp.float32)
        for m in range(materials):
            picked = jnp.where(kind == m, imp[m], picked)
        reflect = (picked - 1.0) / (picked + 1.0)
        reflect_d[at, :] = reflect
        loss = 0.5 * half_scale[at, :] * (1.0 - reflect * reflect)
        loss_d[at, :] = jnp.where(code_d[at, :] < 0, loss, 0.0)
        return carry

    lax.fori_loop(0, groups, reflect_rows, 0)
    for block in range(4):
        yv[block * PAD + SLOT : (block + 1) * PAD, :] = jnp.zeros((PAD - SLOT, elems), jnp.float32)

    def copy_out(section, j):
        return pltpu.make_async_remote_copy(
            src_ref=send_buf.at[pl.ds((section * blocks + j) * SLOT, SLOT), :],
            dst_ref=recv_buf.at[pl.ds((section * blocks + blocks - 1 - j) * SLOT, SLOT), :],
            send_sem=send_sem.at[section, j],
            recv_sem=recv_sem.at[section, blocks - 1 - j],
            device_id=(peers[j],),
            device_id_type=MESH,
        )

    def copy_in(section, j):
        return pltpu.make_async_remote_copy(
            src_ref=send_buf.at[pl.ds((section * blocks + j) * SLOT, SLOT), :],
            dst_ref=recv_buf.at[pl.ds((section * blocks + j) * SLOT, SLOT), :],
            send_sem=send_sem.at[section, j],
            recv_sem=recv_sem.at[section, j],
            device_id=(peers[j],),
            device_id_type=MESH,
        )

    def gather_local(codes):
        high = [code >> 7 for code in codes]
        low = [code & (LANES - 1) for code in codes]
        zero = jnp.zeros((SUB, LANES), jnp.float32)

        def one_row(k, values):
            values = [list(v) for v in values]
            hit = [h == k for h in high]
            for n in range(10):
                row = tab[pl.ds(n * rows + k, 1), :]
                for g in range(len(codes)):
                    values[g][n] = jnp.where(hit[g], lane_pick(row, low[g]), values[g][n])
            return tuple(tuple(v) for v in values)

        def some_rows(q, values):
            for r in range(4):
                values = one_row(q * 4 + r, values)
            return values

        start = tuple(tuple(zero for _ in range(10)) for _ in codes)
        return lax.fori_loop(0, rows // 4, some_rows, start)

    for section in range(2):
        sol_in = sol if section == 0 else sol_out
        reg_in = reg if section == 0 else reg_out

        for field in range(4):
            for first in range(0, 20, SUB):
                count = min(SUB, 20 - first)
                for eb in range(eb_count):
                    place = pl.ds((field * 20 + first) * eb_count + eb, count, stride=eb_count)
                    xd[place, :] = sol_in[
                        field, first : first + count, eb * LANES : (eb + 1) * LANES
                    ]

        for f in range(4):
            normal = [nd[i * rows + f * eb_count : i * rows + (f + 1) * eb_count, :] for i in range(3)]
            for n in range(10):
                node = face_nodes[f][n]
                press, u, v, w = [
                    xd[(field * 20 + node) * eb_count : (field * 20 + node + 1) * eb_count, :]
                    for field in range(4)
                ]
                un = normal[0] * u + normal[1] * v + normal[2] * w
                spot = slice(n * rows + f * eb_count, n * rows + (f + 1) * eb_count)
                tab[spot, :] = press + un
                hd[spot, :] = un - press

        outgoing = gather_local([snd[...]])[0]
        for n in range(10):
            place = pl.ds(section * blocks * SLOT + n, blocks, stride=SLOT)
            send_buf[place, :] = outgoing[n]
        for n in range(10, SLOT):
            place = pl.ds(section * blocks * SLOT + n, blocks, stride=SLOT)
            send_buf[place, :] = jnp.zeros((blocks, LANES), jnp.float32)

        if section == 0:
            expected = sum(v.astype(jnp.int32) for v in valid)
            pl.semaphore_wait(barrier, expected)
        for j in range(blocks):

            @pl.when(valid[j])
            def _():
                copy_out(section, j).start()

        def loss_rows(g, sums):
            at = pl.multiple_of(g * SUB, SUB)
            total = jnp.zeros((SUB, LANES), jnp.float32)
            for n in range(10):
                value = tab[pl.ds(pl.multiple_of(n * rows + at, SUB), SUB), :]
                total = total + value * value
            total = total * loss_d[pl.ds(at, SUB), :]
            kind = mat_d[pl.ds(at, SUB), :]
            return tuple(s + jnp.where(kind == m, total, 0.0) for m, s in enumerate(sums))

        sums = lax.fori_loop(
            0,
            groups,
            loss_rows,
            tuple(jnp.zeros((SUB, LANES), jnp.float32) for _ in range(materials)),
        )
        for m in range(materials):
            tot_out[section * materials + m : section * materials + m + 1, :] = jnp.sum(
                sums[m], axis=0, keepdims=True
            )

        def volume_chunk(c, carry):
            at = pl.ds(pl.multiple_of(c * CHUNK, CHUNK), CHUNK)
            velocity = [sol_in[i + 1, :, at] for i in range(3)]
            metric = geo[:, at]
            for a in range(3):
                yv[a * PAD : a * PAD + 20, at] = (
                    metric[a : a + 1] * velocity[0]
                    + metric[3 + a : 4 + a] * velocity[1]
                    + metric[6 + a : 7 + a] * velocity[2]
                )
            yv[3 * PAD : 3 * PAD + 20, at] = sol_in[0, :, at]
            out = split_dot(vol_high[...], vol_low[...], yv[:, at])
            vol[0:PAD, at] = out[0:PAD]
            grads = [out[(a + 1) * PAD : (a + 2) * PAD] for a in range(3)]
            for i in range(3):
                vol[(i + 1) * PAD : (i + 2) * PAD, at] = -(
                    metric[3 * i : 3 * i + 1] * grads[0]
                    + metric[3 * i + 1 : 3 * i + 2] * grads[1]
                    + metric[3 * i + 2 : 3 * i + 3] * grads[2]
                )
            return carry

        lax.fori_loop(0, elems // CHUNK, volume_chunk, 0)

        def local_pair(q, carry):
            starts = [pl.multiple_of(q * 2 * SUB + g * SUB, SUB) for g in range(2)]
            found = gather_local([code_d[pl.ds(at, SUB), :] for at in starts])
            for at, values in zip(starts, found):
                for n in range(10):
                    acc[pl.ds(pl.multiple_of(n * rows + at, SUB), SUB), :] = values[n]
            return carry

        lax.fori_loop(0, groups // 2, local_pair, 0)

        for j in range(blocks):

            @pl.when(valid[j])
            def _():
                copy_in(section, j).wait_recv()

        def finish_rows(g, carry):
            at = pl.multiple_of(g * SUB, SUB)
            here = pl.ds(at, SUB)
            code = code_d[here, :]
            high = code >> 7
            low = code & (LANES - 1)
            planes = [pl.ds(pl.multiple_of(n * rows + at, SUB), SUB) for n in range(10)]
            values = [acc[planes[n], :] for n in range(10)]
            for j in range(blocks):
                hit = high == rows + j
                for n in range(10):
                    spot = (section * blocks + j) * SLOT + n
                    row = recv_buf[spot : spot + 1, :]
                    values[n] = jnp.where(hit, lane_pick(row, low), values[n])
            turn = orient_d[here, :]
            wall = code < 0
            reflect = reflect_d[here, :]
            scale = half_scale[here, :]
            for n in range(10):
                seen = jnp.where(
                    turn == 0,
                    values[rotations[0][n]],
                    jnp.where(turn == 1, values[rotations[1][n]], values[rotations[2][n]]),
                )
                seen = jnp.where(wall, reflect * tab[planes[n], :], seen)
                hd[planes[n], :] = scale * (hd[planes[n], :] + seen)
            return carry

        lax.fori_loop(0, groups, finish_rows, 0)

        for eb in range(eb_count):
            lanes = slice(eb * LANES, (eb + 1) * LANES)
            normal = [n2[i, :, lanes] for i in range(3)]
            for kb in range(5):
                flux = hd[pl.ds(kb * SUB * eb_count + eb, SUB, stride=eb_count), :]
                fl[kb * SUB : (kb + 1) * SUB, lanes] = flux
                for i in range(3):
                    first = 40 * (i + 1) + kb * SUB
                    fl[first : first + SUB, lanes] = -normal[i] * flux

        def update_chunk(c, carry):
            at = pl.ds(pl.multiple_of(c * CHUNK, CHUNK), CHUNK)
            lifted = split_dot(lift_high[...], lift_low[...], fl[:, at])
            for field in range(4):
                rhs = lifted[field * PAD : field * PAD + 20] + vol[field * PAD : field * PAD + 20, at]
                new = section_decay[section] * reg_in[field, :, at] + time_step * rhs
                sol_out[field, :, at] = sol_in[field, :, at] + section_weight[section] * new
                reg_out[field, :, at] = new
            return carry

        lax.fori_loop(0, elems // CHUNK, update_chunk, 0)

    for section in range(2):
        for j in range(blocks):

            @pl.when(valid[j])
            def _():
                copy_out(section, j).wait_send()


def local(
    solution,
    register,
    geometry,
    normals,
    face_scale,
    impedance,
    neighbour,
    orientation,
    wall_material,
    send_faces,
):
    volume, lift, face_nodes, rotations = operator_tables()
    tables = split_table(volume) + split_table(lift)
    elems = solution.shape[2]
    rows = 4 * elems // LANES
    blocks = send_faces.shape[0]
    materials = impedance.shape[0]
    devices = lax.axis_size("dom")
    f32, i32 = (jnp.float32, jnp.int32)
    vmem = pl.BlockSpec(memory_space=pltpu.VMEM)
    smem = pl.BlockSpec(memory_space=pltpu.SMEM)
    out, register_out, totals = pl.pallas_call(
        functools.partial(step_kernel, devices, face_nodes, rotations),
        out_shape=(
            jax.ShapeDtypeStruct(solution.shape, f32),
            jax.ShapeDtypeStruct(register.shape, f32),
            jax.ShapeDtypeStruct((2 * materials, LANES), f32),
        ),
        in_specs=[vmem] * 5 + [smem] + [vmem] * 8,
        out_specs=(vmem, vmem, vmem),
        scratch_shapes=[
            pltpu.VMEM((20 * rows, LANES), f32),
            pltpu.VMEM((10 * rows, LANES), f32),
            pltpu.VMEM((10 * rows, LANES), f32),
            pltpu.VMEM((10 * rows, LANES), f32),
            pltpu.VMEM((3 * rows, LANES), f32),
            pltpu.VMEM((3, SUB, elems), f32),
            pltpu.VMEM((rows, LANES), i32),
            pltpu.VMEM((rows, LANES), i32),
            pltpu.VMEM((rows, LANES), i32),
            pltpu.VMEM((rows, LANES), f32),
            pltpu.VMEM((rows, LANES), f32),
            pltpu.VMEM((rows, LANES), f32),
            pltpu.VMEM((4 * PAD, elems), f32),
            pltpu.VMEM((4 * PAD, elems), f32),
            pltpu.VMEM((160, elems), f32),
            pltpu.VMEM((2 * blocks * SLOT, LANES), f32),
            pltpu.VMEM((2 * blocks * SLOT, LANES), f32),
            pltpu.SemaphoreType.DMA((2, blocks)),
            pltpu.SemaphoreType.DMA((2, blocks)),
        ],
        compiler_params=pltpu.CompilerParams(
            collective_id=0, has_side_effects=True, vmem_limit_bytes=40 * 1024 * 1024
        ),
    )(
        solution,
        register,
        geometry,
        normals,
        face_scale,
        impedance,
        neighbour,
        orientation,
        wall_material,
        send_faces,
        *tables,
    )
    per_section = jnp.sum(totals, axis=1).reshape(2, materials)
    absorbed = lax.psum(per_section, "dom") * (NMAT / (devices * elems))
    return (out, register_out, absorbed)


def solution(mesh):
    in_specs = (
        P(None, None, "dom"),
        P(None, None, "dom"),
        P(None, "dom"),
        P(None, None, "dom"),
        P(None, "dom"),
        P(),
        P(None, "dom"),
        P(None, "dom"),
        P(None, "dom"),
        P("dom", None),
    )
    out_specs = (P(None, None, "dom"), P(None, None, "dom"), P())
    return jax.shard_map(local, mesh=mesh, in_specs=in_specs, out_specs=out_specs, check_vma=False)
```

```python
import functools
import math

import jax
import jax.numpy as jnp
import numpy as np
from jax import lax
from jax.experimental import pallas as pl
from jax.experimental.pallas import tpu as pltpu
from jax.sharding import PartitionSpec as P

NMAT = 16


section_decay = (-567301805773.0 / 1357537059087.0, -2404267990393.0 / 2016746695238.0)
section_weight = (1720146321549.0 / 2090206949498.0, 3134564353537.0 / 4481467310338.0)
time_step = 0.002


def mat_product(left, right):
    inner = len(right)
    return [
        [sum((left[i][k] * right[k][j] for k in range(inner))) for j in range(len(right[0]))]
        for i in range(len(left))
    ]


def flipped(matrix):
    return [list(row) for row in zip(*matrix)]


def solve_rows(matrix, right):
    size = len(matrix)
    augmented = [list(matrix[i]) + list(right[i]) for i in range(size)]
    for column in range(size):
        pivot = max(range(column, size), key=lambda r: abs(augmented[r][column]))
        augmented[column], augmented[pivot] = (augmented[pivot], augmented[column])
        leader = augmented[column][column]
        augmented[column] = [value / leader for value in augmented[column]]
        for other in range(size):
            if other != column:
                factor = augmented[other][column]
                if factor != 0.0:
                    augmented[other] = [
                        a - factor * b for a, b in zip(augmented[other], augmented[column])
                    ]
    return [row[size:] for row in augmented]


def identity_rows(size):
    return [[1.0 if i == j else 0.0 for j in range(size)] for i in range(size)]


def dg_tables():
    lattice = [(i, j, k) for i in range(4) for j in range(4 - i) for k in range(4 - i - j)]
    coords = [(i / 3.0, j / 3.0, k / 3.0) for i, j, k in lattice]
    vander = [[x**a * y**b * z**c for a, b, c in lattice] for x, y, z in coords]
    inverse = solve_rows(vander, identity_rows(20))
    gradient_rows = []
    for d in range(3):
        derived = []
        for point in coords:
            row = []
            for powers in lattice:
                if powers[d] == 0:
                    row.append(0.0)
                else:
                    lowered = [powers[0], powers[1], powers[2]]
                    lowered[d] = lowered[d] - 1
                    row.append(
                        powers[d]
                        * point[0] ** lowered[0]
                        * point[1] ** lowered[1]
                        * point[2] ** lowered[2]
                    )
            derived.append(row)
        gradient_rows.extend(mat_product(derived, inverse))
    mono_mass = [
        [
            math.factorial(a + p)
            * math.factorial(b + q)
            * math.factorial(c + r)
            / math.factorial(a + b + c + p + q + r + 3)
            for p, q, r in lattice
        ]
        for a, b, c in lattice
    ]
    mass_matrix = mat_product(mat_product(flipped(inverse), mono_mass), inverse)
    plane_points = [(a, b) for a in range(4) for b in range(4 - a)]
    face_coords = [(a / 3.0, b / 3.0) for a, b in plane_points]
    vander_face = [[x**a * y**b for a, b in plane_points] for x, y in face_coords]
    inverse_face = solve_rows(vander_face, identity_rows(10))
    mono_face = [
        [
            math.factorial(a + p) * math.factorial(b + q) / math.factorial(a + b + p + q + 2)
            for p, q in plane_points
        ]
        for a, b in plane_points
    ]
    face_mass = mat_product(mat_product(flipped(inverse_face), mono_face), inverse_face)
    position = {point: n for n, point in enumerate(lattice)}
    builders = [
        lambda a, b: (a, b, 0),
        lambda a, b: (a, 0, b),
        lambda a, b: (0, a, b),
        lambda a, b: (a, b, 3 - a - b),
    ]
    face_nodes = [[position[builder(a, b)] for a, b in plane_points] for builder in builders]
    surface = [[0.0] * 40 for n in range(20)]
    for f in range(4):
        for n in range(10):
            for m in range(10):
                surface[face_nodes[f][n]][f * 10 + m] = face_mass[n][m]
    lift_matrix = solve_rows(mass_matrix, surface)
    rotations = []
    for t in range(3):
        mapping = []
        for a, b in plane_points:
            triple = (b, a, 3 - a - b)
            for s in range(t):
                triple = (triple[1], triple[2], triple[0])
            mapping.append(plane_points.index((triple[0], triple[1])))
        rotations.append(mapping)
    return (gradient_rows, lift_matrix, face_nodes, rotations)


def peer_offsets(half_span):
    return [j - half_span if j < half_span else j - half_span + 1 for j in range(2 * half_span)]


LANES = 128
SUB = 8
PAD = 24
SLOT = 16
CHUNK = 256
MESH = pl.DeviceIdType.MESH


def operator_tables():
    grad_rows, lift_rows, face_nodes, rotations = dg_tables()
    grads = np.array(grad_rows, dtype=np.float64).reshape(3, 20, 20)
    volume = np.zeros((4 * PAD, 4 * PAD))
    for a in range(3):
        volume[0:20, a * PAD : a * PAD + 20] = -grads[a]
        volume[(a + 1) * PAD : (a + 1) * PAD + 20, 3 * PAD : 3 * PAD + 20] = grads[a]
    lift_node_major = np.array(
        [[row[f * 10 + m] for m in range(10) for f in range(4)] for row in lift_rows]
    )
    lift = np.zeros((4 * PAD, 160))
    for field in range(4):
        lift[field * PAD : field * PAD + 20, field * 40 : field * 40 + 40] = lift_node_major
    return (volume, lift, face_nodes, rotations)


def split_table(table):
    single = jnp.asarray(table, dtype=jnp.float32)
    high = single.astype(jnp.bfloat16)
    low = (single - high.astype(jnp.float32)).astype(jnp.bfloat16)
    return (high, low)


def split_dot(high, low, values):
    value_high = values.astype(jnp.bfloat16)
    value_low = (values - value_high.astype(jnp.float32)).astype(jnp.bfloat16)
    dot = functools.partial(jnp.dot, preferred_element_type=jnp.float32)
    return dot(high, value_high) + (dot(high, value_low) + dot(low, value_high))


def lane_pick(row, lanes):
    spread = jnp.broadcast_to(row, lanes.shape)
    return jnp.take_along_axis(spread, lanes, axis=1, mode="promise_in_bounds")


def step_kernel(
    devices,
    face_nodes,
    rotations,
    sol,
    reg,
    geo,
    nrm,
    fsc,
    imp,
    nbr,
    ori,
    mat,
    snd,
    vol_high,
    vol_low,
    lift_high,
    lift_low,
    sol_out,
    reg_out,
    tot_out,
    xd,
    tab,
    hd,
    acc,
    nd,
    n2,
    code_d,
    orient_d,
    mat_d,
    half_scale,
    reflect_d,
    loss_d,
    yv,
    vol,
    fl,
    send_buf,
    recv_buf,
    hot,
    table,
    part_sent,
    part_got,
    send_sem,
    recv_sem,
    part_send_sem,
    part_recv_sem,
):
    elems = sol.shape[2]
    eb_count = elems // LANES
    rows = 4 * eb_count
    groups = rows // SUB
    blocks = snd.shape[0]
    materials = imp.shape[0]
    offsets = peer_offsets(blocks // 2)
    me = lax.axis_index("dom")
    peers = [me + o for o in offsets]
    valid = [(p >= 0) & (p < devices) for p in peers]
    stages = devices.bit_length() - 1
    assert devices == 1 << stages
    partners = [me + (1 << s) - (2 << s) * ((me // (1 << s)) % 2) for s in range(stages)]
    far = [s for s in range(stages) if 1 << s > blocks // 2]

    recv_buf[...] = jnp.zeros_like(recv_buf)
    send_buf[...] = jnp.zeros_like(send_buf)
    barrier = pltpu.get_barrier_semaphore()
    for j in range(blocks):

        @pl.when(valid[j])
        def _():
            pl.semaphore_signal(barrier, inc=1, device_id=(peers[j],), device_id_type=MESH)

    for s in far:
        pl.semaphore_signal(barrier, inc=1, device_id=(partners[s],), device_id_type=MESH)

    for i in range(3):
        n2[i, 0:4, :] = nrm[i]
        n2[i, 4:8, :] = nrm[i]
    for eb in range(eb_count):
        lanes = slice(eb * LANES, (eb + 1) * LANES)
        spread = pl.ds(eb, 4, stride=eb_count)
        for i in range(3):
            nd[pl.ds(i * rows + eb, 4, stride=eb_count), :] = nrm[i, :, lanes]
        half_scale[spread, :] = 0.5 * fsc[:, lanes]
        code_d[spread, :] = nbr[:, lanes]
        orient_d[spread, :] = ori[:, lanes]
        mat_d[spread, :] = mat[:, lanes]

    def reflect_rows(g, carry):
        at = pl.ds(pl.multiple_of(g * SUB, SUB), SUB)
        kind = mat_d[at, :]
        picked = jnp.zeros((SUB, LANES), jnp.float32)
        for m in range(materials):
            picked = jnp.where(kind == m, imp[m], picked)
        reflect = (picked - 1.0) / (picked + 1.0)
        reflect_d[at, :] = reflect
        loss = 0.5 * half_scale[at, :] * (1.0 - reflect * reflect)
        loss_d[at, :] = jnp.where(code_d[at, :] < 0, loss, 0.0)
        return carry

    lax.fori_loop(0, groups, reflect_rows, 0)
    for block in range(4):
        yv[block * PAD + SLOT : (block + 1) * PAD, :] = jnp.zeros((PAD - SLOT, elems), jnp.float32)

    def copy_out(section, j):
        return pltpu.make_async_remote_copy(
            src_ref=send_buf.at[pl.ds((section * blocks + j) * SLOT, SLOT), :],
            dst_ref=recv_buf.at[pl.ds((section * blocks + blocks - 1 - j) * SLOT, SLOT), :],
            send_sem=send_sem.at[section, j],
            recv_sem=recv_sem.at[section, blocks - 1 - j],
            device_id=(peers[j],),
            device_id_type=MESH,
        )

    def copy_in(section, j):
        return pltpu.make_async_remote_copy(
            src_ref=send_buf.at[pl.ds((section * blocks + j) * SLOT, SLOT), :],
            dst_ref=recv_buf.at[pl.ds((section * blocks + j) * SLOT, SLOT), :],
            send_sem=send_sem.at[section, j],
            recv_sem=recv_sem.at[section, j],
            device_id=(peers[j],),
            device_id_type=MESH,
        )

    def hot_rows(codes, column):
        low = jnp.broadcast_to(codes & (LANES - 1), (LANES, LANES))
        one = jnp.where(lax.broadcasted_iota(jnp.int32, (LANES, LANES), 0) == low, 1.0, 0.0)
        one = one.astype(jnp.bfloat16)
        hot[0:LANES, pl.ds(column, LANES)] = one
        hot[LANES : 2 * LANES, pl.ds(column, LANES)] = one

    def hot_face_row(r, carry):
        hot_rows(code_d[pl.ds(r, 1), :], pl.multiple_of(r * LANES, LANES))
        return carry

    lax.fori_loop(0, rows, hot_face_row, 0)
    for j in range(blocks):
        hot_rows(snd[j : j + 1, :], (rows + j) * LANES)

    def fill_table():
        for pair in range(rows // 2):
            value = jnp.concatenate(
                [tab[pl.ds(pair * 2 + h, SUB, stride=rows), :] for h in range(2)], axis=0
            )
            put_split(pair * SLOT, value)
        for q in range(groups):
            value = jnp.concatenate(
                [tab[n * rows + q * SUB : n * rows + (q + 1) * SUB, :] for n in (8, 9)], axis=0
            )
            put_split(rows * SUB + q * SLOT, value)

    def put_split(first, value):
        high = value.astype(jnp.bfloat16)
        table[first : first + SLOT, 0:LANES] = high
        table[first : first + SLOT, LANES : 2 * LANES] = (
            value - high.astype(jnp.float32)
        ).astype(jnp.bfloat16)

    def pick_tile(column, codes):
        product = jnp.dot(
            table[...], hot[:, pl.ds(column, 2 * LANES)], preferred_element_type=jnp.float32
        )
        found = []
        for h in range(2):
            lanes = slice(h * LANES, (h + 1) * LANES)
            high = jnp.broadcast_to(codes[h] >> 7, (SUB, LANES))
            main = jnp.zeros((SUB, LANES), jnp.float32)
            for k in range(rows):
                main = jnp.where(high == k, product[k * SUB : (k + 1) * SUB, lanes], main)
            within = high - lax.broadcasted_iota(jnp.int32, (SUB, LANES), 0)
            rest = [jnp.zeros((SUB, LANES), jnp.float32) for _ in range(2)]
            for q in range(groups):
                hit = within == q * SUB
                for r in range(2):
                    first = rows * SUB + q * SLOT + r * SUB
                    rest[r] = jnp.where(hit, product[first : first + SUB, lanes], rest[r])
            found.append((main, [jnp.sum(r, axis=0, keepdims=True) for r in rest]))
        return found

    def part_copy(s):
        return pltpu.make_async_remote_copy(
            src_ref=part_sent.at[s],
            dst_ref=part_got.at[s],
            send_sem=part_send_sem.at[s],
            recv_sem=part_recv_sem.at[s],
            device_id=(partners[s],),
            device_id_type=MESH,
        )

    def advance(s):
        if s >= stages:
            return
        part_copy(s).wait_recv()
        total = part_sent[s] + part_got[s]
        if s + 1 < stages:
            part_sent[s + 1] = total
            part_copy(s + 1).start()
            return
        ones = jnp.ones((SUB, LANES), jnp.float32)
        for section in range(2):
            sums = lax.dot_general(
                ones,
                total[section * materials : (section + 1) * materials],
                (((1,), (1,)), ((), ())),
                precision=lax.Precision.HIGHEST,
                preferred_element_type=jnp.float32,
            )
            tot_out[section : section + 1, :] = sums[0:1] * (NMAT / (devices * elems))

    for section in range(2):
        sol_in = sol if section == 0 else sol_out
        reg_in = reg if section == 0 else reg_out

        for field in range(4):
            for first in range(0, 20, SUB):
                count = min(SUB, 20 - first)
                for eb in range(eb_count):
                    place = pl.ds((field * 20 + first) * eb_count + eb, count, stride=eb_count)
                    xd[place, :] = sol_in[
                        field, first : first + count, eb * LANES : (eb + 1) * LANES
                    ]

        for f in range(4):
            normal = [nd[i * rows + f * eb_count : i * rows + (f + 1) * eb_count, :] for i in range(3)]
            for n in range(10):
                node = face_nodes[f][n]
                press, u, v, w = [
                    xd[(field * 20 + node) * eb_count : (field * 20 + node + 1) * eb_count, :]
                    for field in range(4)
                ]
                un = normal[0] * u + normal[1] * v + normal[2] * w
                spot = slice(n * rows + f * eb_count, n * rows + (f + 1) * eb_count)
                tab[spot, :] = press + un
                hd[spot, :] = un - press

        fill_table()

        def send_pair(q, carry):
            first = q * 2
            column = pl.multiple_of((rows + first) * LANES, 2 * LANES)
            found = pick_tile(column, [snd[pl.ds(first + h, 1), :] for h in range(2)])
            for h in range(2):
                at = pl.multiple_of((section * blocks + first + h) * SLOT, SLOT)
                main, rest = found[h]
                send_buf[pl.ds(at, SUB), :] = main
                for r in range(2):
                    send_buf[pl.ds(at + SUB + r, 1), :] = rest[r]
            return carry

        lax.fori_loop(0, blocks // 2, send_pair, 0)

        if section == 0:
            expected = len(far) + sum(v.astype(jnp.int32) for v in valid)
            pl.semaphore_wait(barrier, expected)
        for j in range(blocks):

            @pl.when(valid[j])
            def _():
                copy_out(section, j).start()

        def loss_rows(g, sums):
            at = pl.multiple_of(g * SUB, SUB)
            total = jnp.zeros((SUB, LANES), jnp.float32)
            for n in range(10):
                value = tab[pl.ds(pl.multiple_of(n * rows + at, SUB), SUB), :]
                total = total + value * value
            total = total * loss_d[pl.ds(at, SUB), :]
            kind = mat_d[pl.ds(at, SUB), :]
            return tuple(s + jnp.where(kind == m, total, 0.0) for m, s in enumerate(sums))

        sums = lax.fori_loop(
            0,
            groups,
            loss_rows,
            tuple(jnp.zeros((SUB, LANES), jnp.float32) for _ in range(materials)),
        )
        for m in range(materials):
            spot = section * materials + m
            part_sent[0, spot : spot + 1, :] = jnp.sum(sums[m], axis=0, keepdims=True)
        if section == 1:
            part_copy(0).start()

        def volume_chunk(c, carry):
            at = pl.ds(pl.multiple_of(c * CHUNK, CHUNK), CHUNK)
            velocity = [sol_in[i + 1, :, at] for i in range(3)]
            metric = geo[:, at]
            for a in range(3):
                yv[a * PAD : a * PAD + 20, at] = (
                    metric[a : a + 1] * velocity[0]
                    + metric[3 + a : 4 + a] * velocity[1]
                    + metric[6 + a : 7 + a] * velocity[2]
                )
            yv[3 * PAD : 3 * PAD + 20, at] = sol_in[0, :, at]
            out = split_dot(vol_high[...], vol_low[...], yv[:, at])
            vol[0:PAD, at] = out[0:PAD]
            grads = [out[(a + 1) * PAD : (a + 2) * PAD] for a in range(3)]
            for i in range(3):
                vol[(i + 1) * PAD : (i + 2) * PAD, at] = -(
                    metric[3 * i : 3 * i + 1] * grads[0]
                    + metric[3 * i + 1 : 3 * i + 2] * grads[1]
                    + metric[3 * i + 2 : 3 * i + 3] * grads[2]
                )
            return carry

        lax.fori_loop(0, elems // CHUNK, volume_chunk, 0)

        def local_pair(q, carry):
            first = q * 2
            column = pl.multiple_of(first * LANES, 2 * LANES)
            found = pick_tile(column, [code_d[pl.ds(first + h, 1), :] for h in range(2)])
            for h in range(2):
                main, rest = found[h]
                acc[pl.ds(first + h, SUB, stride=rows), :] = main
                for r in range(2):
                    acc[pl.ds((SUB + r) * rows + first + h, 1), :] = rest[r]
            return carry

        if section == 0:
            lax.fori_loop(0, rows // 2, local_pair, 0)
        else:
            advance(0)
            lax.fori_loop(0, rows // 4, local_pair, 0)
            advance(1)
            lax.fori_loop(rows // 4, rows // 2, local_pair, 0)
            advance(2)

        for j in range(blocks):

            @pl.when(valid[j])
            def _():
                copy_in(section, j).wait_recv()

        def finish_rows(g, carry):
            at = pl.multiple_of(g * SUB, SUB)
            here = pl.ds(at, SUB)
            code = code_d[here, :]
            high = code >> 7
            low = code & (LANES - 1)
            planes = [pl.ds(pl.multiple_of(n * rows + at, SUB), SUB) for n in range(10)]
            values = [acc[planes[n], :] for n in range(10)]
            for j in range(blocks):
                hit = high == rows + j
                for n in range(10):
                    spot = (section * blocks + j) * SLOT + n
                    row = recv_buf[spot : spot + 1, :]
                    values[n] = jnp.where(hit, lane_pick(row, low), values[n])
            turn = orient_d[here, :]
            wall = code < 0
            reflect = reflect_d[here, :]
            scale = half_scale[here, :]
            for n in range(10):
                seen = jnp.where(
                    turn == 0,
                    values[rotations[0][n]],
                    jnp.where(turn == 1, values[rotations[1][n]], values[rotations[2][n]]),
                )
                seen = jnp.where(wall, reflect * tab[planes[n], :], seen)
                hd[planes[n], :] = scale * (hd[planes[n], :] + seen)
            return carry

        lax.fori_loop(0, groups, finish_rows, 0)
        if section == 1:
            advance(3)

        for eb in range(eb_count):
            lanes = slice(eb * LANES, (eb + 1) * LANES)
            normal = [n2[i, :, lanes] for i in range(3)]
            for kb in range(5):
                flux = hd[pl.ds(kb * SUB * eb_count + eb, SUB, stride=eb_count), :]
                fl[kb * SUB : (kb + 1) * SUB, lanes] = flux
                for i in range(3):
                    first = 40 * (i + 1) + kb * SUB
                    fl[first : first + SUB, lanes] = -normal[i] * flux

        if section == 1:
            advance(4)

        def update_chunk(c, carry):
            at = pl.ds(pl.multiple_of(c * CHUNK, CHUNK), CHUNK)
            lifted = split_dot(lift_high[...], lift_low[...], fl[:, at])
            for field in range(4):
                rhs = lifted[field * PAD : field * PAD + 20] + vol[field * PAD : field * PAD + 20, at]
                new = section_decay[section] * reg_in[field, :, at] + time_step * rhs
                sol_out[field, :, at] = sol_in[field, :, at] + section_weight[section] * new
                reg_out[field, :, at] = new
            return carry

        lax.fori_loop(0, elems // CHUNK, update_chunk, 0)

    for s in range(5, stages):
        advance(s)
    for s in range(stages):
        part_copy(s).wait_send()

    for section in range(2):
        for j in range(blocks):

            @pl.when(valid[j])
            def _():
                copy_out(section, j).wait_send()


def local(
    solution,
    register,
    geometry,
    normals,
    face_scale,
    impedance,
    neighbour,
    orientation,
    wall_material,
    send_faces,
):
    volume, lift, face_nodes, rotations = operator_tables()
    tables = split_table(volume) + split_table(lift)
    elems = solution.shape[2]
    rows = 4 * elems // LANES
    blocks = send_faces.shape[0]
    materials = impedance.shape[0]
    devices = lax.axis_size("dom")
    stages = devices.bit_length() - 1
    f32, i32 = (jnp.float32, jnp.int32)
    vmem = pl.BlockSpec(memory_space=pltpu.VMEM)
    smem = pl.BlockSpec(memory_space=pltpu.SMEM)
    out, register_out, absorbed = pl.pallas_call(
        functools.partial(step_kernel, devices, face_nodes, rotations),
        out_shape=(
            jax.ShapeDtypeStruct(solution.shape, f32),
            jax.ShapeDtypeStruct(register.shape, f32),
            jax.ShapeDtypeStruct((2, materials), f32),
        ),
        in_specs=[vmem] * 5 + [smem] + [vmem] * 8,
        out_specs=(vmem, vmem, vmem),
        scratch_shapes=[
            pltpu.VMEM((20 * rows, LANES), f32),
            pltpu.VMEM((10 * rows, LANES), f32),
            pltpu.VMEM((10 * rows, LANES), f32),
            pltpu.VMEM((10 * rows, LANES), f32),
            pltpu.VMEM((3 * rows, LANES), f32),
            pltpu.VMEM((3, SUB, elems), f32),
            pltpu.VMEM((rows, LANES), i32),
            pltpu.VMEM((rows, LANES), i32),
            pltpu.VMEM((rows, LANES), i32),
            pltpu.VMEM((rows, LANES), f32),
            pltpu.VMEM((rows, LANES), f32),
            pltpu.VMEM((rows, LANES), f32),
            pltpu.VMEM((4 * PAD, elems), f32),
            pltpu.VMEM((4 * PAD, elems), f32),
            pltpu.VMEM((160, elems), f32),
            pltpu.VMEM((2 * blocks * SLOT, LANES), f32),
            pltpu.VMEM((2 * blocks * SLOT, LANES), f32),
            pltpu.VMEM((2 * LANES, (rows + blocks) * LANES), jnp.bfloat16),
            pltpu.VMEM((10 * rows, 2 * LANES), jnp.bfloat16),
            pltpu.VMEM((stages, 2 * materials, LANES), f32),
            pltpu.VMEM((stages, 2 * materials, LANES), f32),
            pltpu.SemaphoreType.DMA((2, blocks)),
            pltpu.SemaphoreType.DMA((2, blocks)),
            pltpu.SemaphoreType.DMA((stages,)),
            pltpu.SemaphoreType.DMA((stages,)),
        ],
        compiler_params=pltpu.CompilerParams(
            collective_id=0, has_side_effects=True, vmem_limit_bytes=40 * 1024 * 1024
        ),
    )(
        solution,
        register,
        geometry,
        normals,
        face_scale,
        impedance,
        neighbour,
        orientation,
        wall_material,
        send_faces,
        *tables,
    )
    return (out, register_out, absorbed)


def solution(mesh):
    in_specs = (
        P(None, None, "dom"),
        P(None, None, "dom"),
        P(None, "dom"),
        P(None, None, "dom"),
        P(None, "dom"),
        P(),
        P(None, "dom"),
        P(None, "dom"),
        P(None, "dom"),
        P("dom", None),
    )
    out_specs = (P(None, None, "dom"), P(None, None, "dom"), P())
    return jax.shard_map(local, mesh=mesh, in_specs=in_specs, out_specs=out_specs, check_vma=False)
```

```python
import functools
import math

import jax
import jax.numpy as jnp
import numpy as np
from jax import lax
from jax.experimental import pallas as pl
from jax.experimental.pallas import tpu as pltpu
from jax.sharding import PartitionSpec as P

NMAT = 16


section_decay = (-567301805773.0 / 1357537059087.0, -2404267990393.0 / 2016746695238.0)
section_weight = (1720146321549.0 / 2090206949498.0, 3134564353537.0 / 4481467310338.0)
time_step = 0.002


def mat_product(left, right):
    inner = len(right)
    return [
        [sum((left[i][k] * right[k][j] for k in range(inner))) for j in range(len(right[0]))]
        for i in range(len(left))
    ]


def flipped(matrix):
    return [list(row) for row in zip(*matrix)]


def solve_rows(matrix, right):
    size = len(matrix)
    augmented = [list(matrix[i]) + list(right[i]) for i in range(size)]
    for column in range(size):
        pivot = max(range(column, size), key=lambda r: abs(augmented[r][column]))
        augmented[column], augmented[pivot] = (augmented[pivot], augmented[column])
        leader = augmented[column][column]
        augmented[column] = [value / leader for value in augmented[column]]
        for other in range(size):
            if other != column:
                factor = augmented[other][column]
                if factor != 0.0:
                    augmented[other] = [
                        a - factor * b for a, b in zip(augmented[other], augmented[column])
                    ]
    return [row[size:] for row in augmented]


def identity_rows(size):
    return [[1.0 if i == j else 0.0 for j in range(size)] for i in range(size)]


def dg_tables():
    lattice = [(i, j, k) for i in range(4) for j in range(4 - i) for k in range(4 - i - j)]
    coords = [(i / 3.0, j / 3.0, k / 3.0) for i, j, k in lattice]
    vander = [[x**a * y**b * z**c for a, b, c in lattice] for x, y, z in coords]
    inverse = solve_rows(vander, identity_rows(20))
    gradient_rows = []
    for d in range(3):
        derived = []
        for point in coords:
            row = []
            for powers in lattice:
                if powers[d] == 0:
                    row.append(0.0)
                else:
                    lowered = [powers[0], powers[1], powers[2]]
                    lowered[d] = lowered[d] - 1
                    row.append(
                        powers[d]
                        * point[0] ** lowered[0]
                        * point[1] ** lowered[1]
                        * point[2] ** lowered[2]
                    )
            derived.append(row)
        gradient_rows.extend(mat_product(derived, inverse))
    mono_mass = [
        [
            math.factorial(a + p)
            * math.factorial(b + q)
            * math.factorial(c + r)
            / math.factorial(a + b + c + p + q + r + 3)
            for p, q, r in lattice
        ]
        for a, b, c in lattice
    ]
    mass_matrix = mat_product(mat_product(flipped(inverse), mono_mass), inverse)
    plane_points = [(a, b) for a in range(4) for b in range(4 - a)]
    face_coords = [(a / 3.0, b / 3.0) for a, b in plane_points]
    vander_face = [[x**a * y**b for a, b in plane_points] for x, y in face_coords]
    inverse_face = solve_rows(vander_face, identity_rows(10))
    mono_face = [
        [
            math.factorial(a + p) * math.factorial(b + q) / math.factorial(a + b + p + q + 2)
            for p, q in plane_points
        ]
        for a, b in plane_points
    ]
    face_mass = mat_product(mat_product(flipped(inverse_face), mono_face), inverse_face)
    position = {point: n for n, point in enumerate(lattice)}
    builders = [
        lambda a, b: (a, b, 0),
        lambda a, b: (a, 0, b),
        lambda a, b: (0, a, b),
        lambda a, b: (a, b, 3 - a - b),
    ]
    face_nodes = [[position[builder(a, b)] for a, b in plane_points] for builder in builders]
    surface = [[0.0] * 40 for n in range(20)]
    for f in range(4):
        for n in range(10):
            for m in range(10):
                surface[face_nodes[f][n]][f * 10 + m] = face_mass[n][m]
    lift_matrix = solve_rows(mass_matrix, surface)
    rotations = []
    for t in range(3):
        mapping = []
        for a, b in plane_points:
            triple = (b, a, 3 - a - b)
            for s in range(t):
                triple = (triple[1], triple[2], triple[0])
            mapping.append(plane_points.index((triple[0], triple[1])))
        rotations.append(mapping)
    return (gradient_rows, lift_matrix, face_nodes, rotations)


def peer_offsets(half_span):
    return [j - half_span if j < half_span else j - half_span + 1 for j in range(2 * half_span)]


LANES = 128
SUB = 8
PAD = 24
SLOT = 16
CHUNK = 256
MESH = pl.DeviceIdType.MESH


def operator_tables():
    grad_rows, lift_rows, face_nodes, rotations = dg_tables()
    grads = np.array(grad_rows, dtype=np.float64).reshape(3, 20, 20)
    volume = np.zeros((4 * PAD, 4 * PAD))
    for a in range(3):
        volume[0:20, a * PAD : a * PAD + 20] = -grads[a]
        volume[(a + 1) * PAD : (a + 1) * PAD + 20, 3 * PAD : 3 * PAD + 20] = grads[a]
    lift_node_major = np.array(
        [[row[f * 10 + m] for m in range(10) for f in range(4)] for row in lift_rows]
    )
    lift = np.zeros((4 * PAD, 160))
    for field in range(4):
        lift[field * PAD : field * PAD + 20, field * 40 : field * 40 + 40] = lift_node_major
    return (volume, lift, face_nodes, rotations)


def split_table(table):
    single = jnp.asarray(table, dtype=jnp.float32)
    high = single.astype(jnp.bfloat16)
    low = (single - high.astype(jnp.float32)).astype(jnp.bfloat16)
    return jnp.concatenate([high, high, low], axis=1)


def split_dot(parts, values):
    high = values.astype(jnp.bfloat16)
    low = (values - high.astype(jnp.float32)).astype(jnp.bfloat16)
    stacked = jnp.concatenate([high, low, high], axis=0)
    return jnp.dot(parts, stacked, preferred_element_type=jnp.float32)


def lane_pick(row, lanes):
    spread = jnp.broadcast_to(row, lanes.shape)
    return jnp.take_along_axis(spread, lanes, axis=1, mode="promise_in_bounds")


def step_kernel(
    devices,
    face_nodes,
    rotations,
    sol,
    reg,
    geo,
    nrm,
    fsc,
    imp,
    nbr,
    ori,
    mat,
    snd,
    vol_parts,
    lift_parts,
    sol_out,
    reg_out,
    tot_out,
    xd,
    tab,
    hd,
    acc,
    nd,
    n2,
    code_d,
    orient_d,
    mat_d,
    half_scale,
    reflect_d,
    loss_d,
    yv,
    vol,
    fl,
    send_buf,
    recv_buf,
    hot,
    table,
    part_sent,
    part_got,
    send_sem,
    recv_sem,
    part_send_sem,
    part_recv_sem,
):
    elems = sol.shape[2]
    eb_count = elems // LANES
    rows = 4 * eb_count
    groups = rows // SUB
    blocks = snd.shape[0]
    materials = imp.shape[0]
    offsets = peer_offsets(blocks // 2)
    me = lax.axis_index("dom")
    peers = [me + o for o in offsets]
    valid = [(p >= 0) & (p < devices) for p in peers]
    stages = devices.bit_length() - 1
    assert devices == 1 << stages
    partners = [me + (1 << s) - (2 << s) * ((me // (1 << s)) % 2) for s in range(stages)]
    far = [s for s in range(stages) if 1 << s > blocks // 2]

    recv_buf[...] = jnp.zeros_like(recv_buf)
    send_buf[...] = jnp.zeros_like(send_buf)
    barrier = pltpu.get_barrier_semaphore()
    for j in range(blocks):

        @pl.when(valid[j])
        def _():
            pl.semaphore_signal(barrier, inc=1, device_id=(peers[j],), device_id_type=MESH)

    for s in far:
        pl.semaphore_signal(barrier, inc=1, device_id=(partners[s],), device_id_type=MESH)

    for i in range(3):
        n2[i, 0:4, :] = nrm[i]
        n2[i, 4:8, :] = nrm[i]
    for eb in range(eb_count):
        lanes = slice(eb * LANES, (eb + 1) * LANES)
        spread = pl.ds(eb, 4, stride=eb_count)
        for i in range(3):
            nd[pl.ds(i * rows + eb, 4, stride=eb_count), :] = nrm[i, :, lanes]
        half_scale[spread, :] = 0.5 * fsc[:, lanes]
        code_d[spread, :] = nbr[:, lanes]
        orient_d[spread, :] = ori[:, lanes]
        mat_d[spread, :] = mat[:, lanes]

    def reflect_rows(g, carry):
        at = pl.ds(pl.multiple_of(g * SUB, SUB), SUB)
        kind = mat_d[at, :]
        picked = jnp.zeros((SUB, LANES), jnp.float32)
        for m in range(materials):
            picked = jnp.where(kind == m, imp[m], picked)
        reflect = (picked - 1.0) / (picked + 1.0)
        reflect_d[at, :] = reflect
        loss = 0.5 * half_scale[at, :] * (1.0 - reflect * reflect)
        loss_d[at, :] = jnp.where(code_d[at, :] < 0, loss, 0.0)
        return carry

    lax.fori_loop(0, groups, reflect_rows, 0)
    for block in range(4):
        yv[block * PAD + SLOT : (block + 1) * PAD, :] = jnp.zeros((PAD - SLOT, elems), jnp.float32)

    def copy_out(section, j):
        return pltpu.make_async_remote_copy(
            src_ref=send_buf.at[pl.ds((section * blocks + j) * SLOT, SLOT), :],
            dst_ref=recv_buf.at[pl.ds((section * blocks + blocks - 1 - j) * SLOT, SLOT), :],
            send_sem=send_sem.at[section, j],
            recv_sem=recv_sem.at[section, blocks - 1 - j],
            device_id=(peers[j],),
            device_id_type=MESH,
        )

    def copy_in(section, j):
        return pltpu.make_async_remote_copy(
            src_ref=send_buf.at[pl.ds((section * blocks + j) * SLOT, SLOT), :],
            dst_ref=recv_buf.at[pl.ds((section * blocks + j) * SLOT, SLOT), :],
            send_sem=send_sem.at[section, j],
            recv_sem=recv_sem.at[section, j],
            device_id=(peers[j],),
            device_id_type=MESH,
        )

    def hot_rows(codes, column):
        low = jnp.broadcast_to(codes & (LANES - 1), (LANES, LANES))
        one = jnp.where(lax.broadcasted_iota(jnp.int32, (LANES, LANES), 0) == low, 1.0, 0.0)
        one = one.astype(jnp.bfloat16)
        hot[0:LANES, pl.ds(column, LANES)] = one
        hot[LANES : 2 * LANES, pl.ds(column, LANES)] = one

    def hot_face_row(r, carry):
        hot_rows(code_d[pl.ds(r, 1), :], pl.multiple_of(r * LANES, LANES))
        return carry

    lax.fori_loop(0, rows, hot_face_row, 0)
    for j in range(blocks):
        hot_rows(snd[j : j + 1, :], (rows + j) * LANES)

    def fill_table():
        for pair in range(rows // 2):
            value = jnp.concatenate(
                [tab[pl.ds(pair * 2 + h, SUB, stride=rows), :] for h in range(2)], axis=0
            )
            put_split(pair * SLOT, value)
        for q in range(groups):
            value = jnp.concatenate(
                [tab[n * rows + q * SUB : n * rows + (q + 1) * SUB, :] for n in (8, 9)], axis=0
            )
            put_split(rows * SUB + q * SLOT, value)

    def put_split(first, value):
        high = value.astype(jnp.bfloat16)
        table[first : first + SLOT, 0:LANES] = high
        table[first : first + SLOT, LANES : 2 * LANES] = (
            value - high.astype(jnp.float32)
        ).astype(jnp.bfloat16)

    def pick_tile(column, codes):
        product = jnp.dot(
            table[...], hot[:, pl.ds(column, 2 * LANES)], preferred_element_type=jnp.float32
        )
        found = []
        for h in range(2):
            lanes = slice(h * LANES, (h + 1) * LANES)
            high = jnp.broadcast_to(codes[h] >> 7, (SUB, LANES))
            main = jnp.zeros((SUB, LANES), jnp.float32)
            for k in range(rows):
                main = jnp.where(high == k, product[k * SUB : (k + 1) * SUB, lanes], main)
            within = high - lax.broadcasted_iota(jnp.int32, (SUB, LANES), 0)
            rest = [jnp.zeros((SUB, LANES), jnp.float32) for _ in range(2)]
            for q in range(groups):
                hit = within == q * SUB
                for r in range(2):
                    first = rows * SUB + q * SLOT + r * SUB
                    rest[r] = jnp.where(hit, product[first : first + SUB, lanes], rest[r])
            found.append((main, [jnp.sum(r, axis=0, keepdims=True) for r in rest]))
        return found

    def part_copy(s):
        return pltpu.make_async_remote_copy(
            src_ref=part_sent.at[s],
            dst_ref=part_got.at[s],
            send_sem=part_send_sem.at[s],
            recv_sem=part_recv_sem.at[s],
            device_id=(partners[s],),
            device_id_type=MESH,
        )

    def advance(s):
        if s >= stages:
            return
        part_copy(s).wait_recv()
        total = part_sent[s] + part_got[s]
        if s + 1 < stages:
            part_sent[s + 1] = total
            part_copy(s + 1).start()
            return
        ones = jnp.ones((SUB, LANES), jnp.float32)
        for section in range(2):
            sums = lax.dot_general(
                ones,
                total[section * materials : (section + 1) * materials],
                (((1,), (1,)), ((), ())),
                precision=lax.Precision.HIGHEST,
                preferred_element_type=jnp.float32,
            )
            tot_out[section : section + 1, :] = sums[0:1] * (NMAT / (devices * elems))

    for section in range(2):
        sol_in = sol if section == 0 else sol_out
        reg_in = reg if section == 0 else reg_out

        for field in range(4):
            for first in range(0, 20, SUB):
                count = min(SUB, 20 - first)
                for eb in range(eb_count):
                    place = pl.ds((field * 20 + first) * eb_count + eb, count, stride=eb_count)
                    xd[place, :] = sol_in[
                        field, first : first + count, eb * LANES : (eb + 1) * LANES
                    ]

        for f in range(4):
            normal = [nd[i * rows + f * eb_count : i * rows + (f + 1) * eb_count, :] for i in range(3)]
            for n in range(10):
                node = face_nodes[f][n]
                press, u, v, w = [
                    xd[(field * 20 + node) * eb_count : (field * 20 + node + 1) * eb_count, :]
                    for field in range(4)
                ]
                un = normal[0] * u + normal[1] * v + normal[2] * w
                spot = slice(n * rows + f * eb_count, n * rows + (f + 1) * eb_count)
                tab[spot, :] = press + un
                hd[spot, :] = un - press

        fill_table()

        def send_pair(q, carry):
            first = q * 2
            column = pl.multiple_of((rows + first) * LANES, 2 * LANES)
            found = pick_tile(column, [snd[pl.ds(first + h, 1), :] for h in range(2)])
            for h in range(2):
                at = pl.multiple_of((section * blocks + first + h) * SLOT, SLOT)
                main, rest = found[h]
                send_buf[pl.ds(at, SUB), :] = main
                for r in range(2):
                    send_buf[pl.ds(at + SUB + r, 1), :] = rest[r]
            return carry

        lax.fori_loop(0, blocks // 2, send_pair, 0)

        if section == 0:
            expected = len(far) + sum(v.astype(jnp.int32) for v in valid)
            pl.semaphore_wait(barrier, expected)
        for j in range(blocks):

            @pl.when(valid[j])
            def _():
                copy_out(section, j).start()

        def loss_rows(g, sums):
            at = pl.multiple_of(g * SUB, SUB)
            total = jnp.zeros((SUB, LANES), jnp.float32)
            for n in range(10):
                value = tab[pl.ds(pl.multiple_of(n * rows + at, SUB), SUB), :]
                total = total + value * value
            total = total * loss_d[pl.ds(at, SUB), :]
            kind = mat_d[pl.ds(at, SUB), :]
            return tuple(s + jnp.where(kind == m, total, 0.0) for m, s in enumerate(sums))

        sums = lax.fori_loop(
            0,
            groups,
            loss_rows,
            tuple(jnp.zeros((SUB, LANES), jnp.float32) for _ in range(materials)),
        )
        for m in range(materials):
            spot = section * materials + m
            part_sent[0, spot : spot + 1, :] = jnp.sum(sums[m], axis=0, keepdims=True)
        if section == 1:
            part_copy(0).start()

        def volume_chunk(c):
            at = pl.ds(pl.multiple_of(c * CHUNK, CHUNK), CHUNK)
            velocity = [sol_in[i + 1, :, at] for i in range(3)]
            metric = geo[:, at]
            for a in range(3):
                yv[a * PAD : a * PAD + 20, at] = (
                    metric[a : a + 1] * velocity[0]
                    + metric[3 + a : 4 + a] * velocity[1]
                    + metric[6 + a : 7 + a] * velocity[2]
                )
            yv[3 * PAD : 3 * PAD + 20, at] = sol_in[0, :, at]
            out = split_dot(vol_parts[...], yv[:, at])
            vol[0:PAD, at] = out[0:PAD]
            grads = [out[(a + 1) * PAD : (a + 2) * PAD] for a in range(3)]
            for i in range(3):
                vol[(i + 1) * PAD : (i + 2) * PAD, at] = -(
                    metric[3 * i : 3 * i + 1] * grads[0]
                    + metric[3 * i + 1 : 3 * i + 2] * grads[1]
                    + metric[3 * i + 2 : 3 * i + 3] * grads[2]
                )

        def matmul_pair(q):
            first = q * 2
            column = pl.multiple_of(first * LANES, 2 * LANES)
            found = pick_tile(column, [code_d[pl.ds(first + h, 1), :] for h in range(2)])
            for h in range(2):
                main, rest = found[h]
                acc[pl.ds(first + h, SUB, stride=rows), :] = main
                for r in range(2):
                    acc[pl.ds((SUB + r) * rows + first + h, 1), :] = rest[r]

        def pick_rows(at, start, count):
            at = pl.multiple_of(at, SUB)
            planes = [pl.ds(pl.multiple_of(n * rows + at, SUB), SUB) for n in range(10)]
            code = code_d[pl.ds(at, SUB), :]
            high = (code >> 7) - start
            low = code & (LANES - 1)
            values = [acc[plane, :] for plane in planes]
            for k in range(count):
                hit = high == k
                for n in range(10):
                    row = tab[pl.ds(n * rows + start + k, 1), :]
                    values[n] = jnp.where(hit, lane_pick(row, low), values[n])
            for n in range(10):
                acc[planes[n], :] = values[n]

        def local_step(i, carry):
            volume_chunk(i)
            matmul_pair(2 * i)
            matmul_pair(2 * i + 1)
            pick_rows(rows // 2 + (i // 2) * SUB, (i % 2) * (rows // 2), rows // 2)
            return carry

        for n in range(10):
            half = slice(n * rows + rows // 2, (n + 1) * rows)
            acc[half, :] = jnp.zeros((rows // 2, LANES), jnp.float32)
        if section == 0:
            lax.fori_loop(0, groups, local_step, 0)
        else:
            lax.fori_loop(0, groups // 2, local_step, 0)
            advance(0)
            lax.fori_loop(groups // 2, groups, local_step, 0)
            advance(1)

        for j in range(blocks):

            @pl.when(valid[j])
            def _():
                copy_in(section, j).wait_recv()

        def finish_rows(g, carry):
            at = pl.multiple_of(g * SUB, SUB)
            here = pl.ds(at, SUB)
            code = code_d[here, :]
            high = code >> 7
            low = code & (LANES - 1)
            planes = [pl.ds(pl.multiple_of(n * rows + at, SUB), SUB) for n in range(10)]
            values = [acc[planes[n], :] for n in range(10)]
            for j in range(blocks):
                hit = high == rows + j
                for n in range(10):
                    spot = (section * blocks + j) * SLOT + n
                    row = recv_buf[spot : spot + 1, :]
                    values[n] = jnp.where(hit, lane_pick(row, low), values[n])
            turn = orient_d[here, :]
            wall = code < 0
            reflect = reflect_d[here, :]
            scale = half_scale[here, :]
            for n in range(10):
                seen = jnp.where(
                    turn == 0,
                    values[rotations[0][n]],
                    jnp.where(turn == 1, values[rotations[1][n]], values[rotations[2][n]]),
                )
                seen = jnp.where(wall, reflect * tab[planes[n], :], seen)
                hd[planes[n], :] = scale * (hd[planes[n], :] + seen)
            return carry

        lax.fori_loop(0, groups, finish_rows, 0)
        if section == 1:
            advance(2)

        for eb in range(eb_count):
            lanes = slice(eb * LANES, (eb + 1) * LANES)
            normal = [n2[i, :, lanes] for i in range(3)]
            for kb in range(5):
                flux = hd[pl.ds(kb * SUB * eb_count + eb, SUB, stride=eb_count), :]
                fl[kb * SUB : (kb + 1) * SUB, lanes] = flux
                for i in range(3):
                    first = 40 * (i + 1) + kb * SUB
                    fl[first : first + SUB, lanes] = -normal[i] * flux

        if section == 1:
            advance(3)

        def update_chunk(c, carry):
            at = pl.ds(pl.multiple_of(c * CHUNK, CHUNK), CHUNK)
            lifted = split_dot(lift_parts[...], fl[:, at])
            for field in range(4):
                rhs = lifted[field * PAD : field * PAD + 20] + vol[field * PAD : field * PAD + 20, at]
                new = section_decay[section] * reg_in[field, :, at] + time_step * rhs
                sol_out[field, :, at] = sol_in[field, :, at] + section_weight[section] * new
                reg_out[field, :, at] = new
            return carry

        lax.fori_loop(0, elems // CHUNK, update_chunk, 0, unroll=4)

    for s in range(4, stages):
        advance(s)
    for s in range(stages):
        part_copy(s).wait_send()

    for section in range(2):
        for j in range(blocks):

            @pl.when(valid[j])
            def _():
                copy_out(section, j).wait_send()


def local(
    solution,
    register,
    geometry,
    normals,
    face_scale,
    impedance,
    neighbour,
    orientation,
    wall_material,
    send_faces,
):
    volume, lift, face_nodes, rotations = operator_tables()
    tables = (split_table(volume), split_table(lift))
    elems = solution.shape[2]
    rows = 4 * elems // LANES
    blocks = send_faces.shape[0]
    materials = impedance.shape[0]
    devices = lax.axis_size("dom")
    stages = devices.bit_length() - 1
    f32, i32 = (jnp.float32, jnp.int32)
    vmem = pl.BlockSpec(memory_space=pltpu.VMEM)
    smem = pl.BlockSpec(memory_space=pltpu.SMEM)
    out, register_out, absorbed = pl.pallas_call(
        functools.partial(step_kernel, devices, face_nodes, rotations),
        out_shape=(
            jax.ShapeDtypeStruct(solution.shape, f32),
            jax.ShapeDtypeStruct(register.shape, f32),
            jax.ShapeDtypeStruct((2, materials), f32),
        ),
        in_specs=[vmem] * 5 + [smem] + [vmem] * 6,
        out_specs=(vmem, vmem, vmem),
        scratch_shapes=[
            pltpu.VMEM((20 * rows, LANES), f32),
            pltpu.VMEM((10 * rows, LANES), f32),
            pltpu.VMEM((10 * rows, LANES), f32),
            pltpu.VMEM((10 * rows, LANES), f32),
            pltpu.VMEM((3 * rows, LANES), f32),
            pltpu.VMEM((3, SUB, elems), f32),
            pltpu.VMEM((rows, LANES), i32),
            pltpu.VMEM((rows, LANES), i32),
            pltpu.VMEM((rows, LANES), i32),
            pltpu.VMEM((rows, LANES), f32),
            pltpu.VMEM((rows, LANES), f32),
            pltpu.VMEM((rows, LANES), f32),
            pltpu.VMEM((4 * PAD, elems), f32),
            pltpu.VMEM((4 * PAD, elems), f32),
            pltpu.VMEM((160, elems), f32),
            pltpu.VMEM((2 * blocks * SLOT, LANES), f32),
            pltpu.VMEM((2 * blocks * SLOT, LANES), f32),
            pltpu.VMEM((2 * LANES, (rows + blocks) * LANES), jnp.bfloat16),
            pltpu.VMEM((10 * rows, 2 * LANES), jnp.bfloat16),
            pltpu.VMEM((stages, 2 * materials, LANES), f32),
            pltpu.VMEM((stages, 2 * materials, LANES), f32),
            pltpu.SemaphoreType.DMA((2, blocks)),
            pltpu.SemaphoreType.DMA((2, blocks)),
            pltpu.SemaphoreType.DMA((stages,)),
            pltpu.SemaphoreType.DMA((stages,)),
        ],
        compiler_params=pltpu.CompilerParams(
            collective_id=0, has_side_effects=True, vmem_limit_bytes=40 * 1024 * 1024
        ),
    )(
        solution,
        register,
        geometry,
        normals,
        face_scale,
        impedance,
        neighbour,
        orientation,
        wall_material,
        send_faces,
        *tables,
    )
    return (out, register_out, absorbed)


def solution(mesh):
    in_specs = (
        P(None, None, "dom"),
        P(None, None, "dom"),
        P(None, "dom"),
        P(None, None, "dom"),
        P(None, "dom"),
        P(),
        P(None, "dom"),
        P(None, "dom"),
        P(None, "dom"),
        P("dom", None),
    )
    out_specs = (P(None, None, "dom"), P(None, None, "dom"), P())
    return jax.shard_map(local, mesh=mesh, in_specs=in_specs, out_specs=out_specs, check_vma=False)
```

```python
import functools
import math

import jax
import jax.numpy as jnp
import numpy as np
from jax import lax
from jax.experimental import pallas as pl
from jax.experimental.pallas import tpu as pltpu
from jax.sharding import PartitionSpec as P

NMAT = 16


section_decay = (-567301805773.0 / 1357537059087.0, -2404267990393.0 / 2016746695238.0)
section_weight = (1720146321549.0 / 2090206949498.0, 3134564353537.0 / 4481467310338.0)
time_step = 0.002


def mat_product(left, right):
    inner = len(right)
    return [
        [sum((left[i][k] * right[k][j] for k in range(inner))) for j in range(len(right[0]))]
        for i in range(len(left))
    ]


def flipped(matrix):
    return [list(row) for row in zip(*matrix)]


def solve_rows(matrix, right):
    size = len(matrix)
    augmented = [list(matrix[i]) + list(right[i]) for i in range(size)]
    for column in range(size):
        pivot = max(range(column, size), key=lambda r: abs(augmented[r][column]))
        augmented[column], augmented[pivot] = (augmented[pivot], augmented[column])
        leader = augmented[column][column]
        augmented[column] = [value / leader for value in augmented[column]]
        for other in range(size):
            if other != column:
                factor = augmented[other][column]
                if factor != 0.0:
                    augmented[other] = [
                        a - factor * b for a, b in zip(augmented[other], augmented[column])
                    ]
    return [row[size:] for row in augmented]


def identity_rows(size):
    return [[1.0 if i == j else 0.0 for j in range(size)] for i in range(size)]


def dg_tables():
    lattice = [(i, j, k) for i in range(4) for j in range(4 - i) for k in range(4 - i - j)]
    coords = [(i / 3.0, j / 3.0, k / 3.0) for i, j, k in lattice]
    vander = [[x**a * y**b * z**c for a, b, c in lattice] for x, y, z in coords]
    inverse = solve_rows(vander, identity_rows(20))
    gradient_rows = []
    for d in range(3):
        derived = []
        for point in coords:
            row = []
            for powers in lattice:
                if powers[d] == 0:
                    row.append(0.0)
                else:
                    lowered = [powers[0], powers[1], powers[2]]
                    lowered[d] = lowered[d] - 1
                    row.append(
                        powers[d]
                        * point[0] ** lowered[0]
                        * point[1] ** lowered[1]
                        * point[2] ** lowered[2]
                    )
            derived.append(row)
        gradient_rows.extend(mat_product(derived, inverse))
    mono_mass = [
        [
            math.factorial(a + p)
            * math.factorial(b + q)
            * math.factorial(c + r)
            / math.factorial(a + b + c + p + q + r + 3)
            for p, q, r in lattice
        ]
        for a, b, c in lattice
    ]
    mass_matrix = mat_product(mat_product(flipped(inverse), mono_mass), inverse)
    plane_points = [(a, b) for a in range(4) for b in range(4 - a)]
    face_coords = [(a / 3.0, b / 3.0) for a, b in plane_points]
    vander_face = [[x**a * y**b for a, b in plane_points] for x, y in face_coords]
    inverse_face = solve_rows(vander_face, identity_rows(10))
    mono_face = [
        [
            math.factorial(a + p) * math.factorial(b + q) / math.factorial(a + b + p + q + 2)
            for p, q in plane_points
        ]
        for a, b in plane_points
    ]
    face_mass = mat_product(mat_product(flipped(inverse_face), mono_face), inverse_face)
    position = {point: n for n, point in enumerate(lattice)}
    builders = [
        lambda a, b: (a, b, 0),
        lambda a, b: (a, 0, b),
        lambda a, b: (0, a, b),
        lambda a, b: (a, b, 3 - a - b),
    ]
    face_nodes = [[position[builder(a, b)] for a, b in plane_points] for builder in builders]
    surface = [[0.0] * 40 for n in range(20)]
    for f in range(4):
        for n in range(10):
            for m in range(10):
                surface[face_nodes[f][n]][f * 10 + m] = face_mass[n][m]
    lift_matrix = solve_rows(mass_matrix, surface)
    rotations = []
    for t in range(3):
        mapping = []
        for a, b in plane_points:
            triple = (b, a, 3 - a - b)
            for s in range(t):
                triple = (triple[1], triple[2], triple[0])
            mapping.append(plane_points.index((triple[0], triple[1])))
        rotations.append(mapping)
    return (gradient_rows, lift_matrix, face_nodes, rotations)


def peer_offsets(half_span):
    return [j - half_span if j < half_span else j - half_span + 1 for j in range(2 * half_span)]


LANES = 128
SUB = 8
PAD = 24
SLOT = 16
CHUNK = 256
MESH = pl.DeviceIdType.MESH


def operator_tables():
    grad_rows, lift_rows, face_nodes, rotations = dg_tables()
    grads = np.array(grad_rows, dtype=np.float64).reshape(3, 20, 20)
    volume = np.zeros((80, 12 * PAD))
    for a in range(3):
        volume[0::4, a * PAD : a * PAD + 20] = -grads[a]
        for i in range(3):
            first = (3 + 3 * i + a) * PAD
            volume[i + 1 :: 4, first : first + 20] = -grads[a]
    lift_node_major = np.array(
        [[row[f * 10 + m] for m in range(10) for f in range(4)] for row in lift_rows]
    )
    lift = np.zeros((80, 160))
    for field in range(4):
        lift[field::4, field * 40 : field * 40 + 40] = lift_node_major
    return (volume, lift, face_nodes, rotations)


def split_table(table):
    single = jnp.asarray(table, dtype=jnp.float32)
    high = single.astype(jnp.bfloat16)
    low = (single - high.astype(jnp.float32)).astype(jnp.bfloat16)
    return jnp.concatenate([high, high, low], axis=1)


def split_dot(parts, values):
    high = values.astype(jnp.bfloat16)
    low = (values - high.astype(jnp.float32)).astype(jnp.bfloat16)
    stacked = jnp.concatenate([high, low, high], axis=0)
    return jnp.dot(parts, stacked, preferred_element_type=jnp.float32)


def lane_pick(source, lanes):
    return jnp.take_along_axis(source, lanes, axis=1, mode="promise_in_bounds")


def step_kernel(
    devices,
    face_nodes,
    rotations,
    sol,
    reg,
    geo,
    nrm,
    fsc,
    imp,
    nbr,
    ori,
    mat,
    snd,
    vol_parts,
    lift_parts,
    sol_out,
    reg_out,
    tot_out,
    xd,
    tab,
    hd,
    acc,
    nd,
    n2,
    code_d,
    orient_d,
    mat_d,
    half_scale,
    reflect_d,
    loss_d,
    nat,
    vol,
    fl,
    send_buf,
    recv_buf,
    hot,
    table,
    spread_tab,
    spread_recv,
    part_sent,
    part_got,
    send_sem,
    recv_sem,
    part_send_sem,
    part_recv_sem,
):
    elems = sol.shape[2]
    eb_count = elems // LANES
    rows = 4 * eb_count
    groups = rows // SUB
    blocks = snd.shape[0]
    materials = imp.shape[0]
    offsets = peer_offsets(blocks // 2)
    me = lax.axis_index("dom")
    peers = [me + o for o in offsets]
    valid = [(p >= 0) & (p < devices) for p in peers]
    stages = devices.bit_length() - 1
    assert devices == 1 << stages
    partners = [me + (1 << s) - (2 << s) * ((me // (1 << s)) % 2) for s in range(stages)]
    far = [s for s in range(stages) if 1 << s > blocks // 2]

    recv_buf[...] = jnp.zeros_like(recv_buf)
    send_buf[...] = jnp.zeros_like(send_buf)
    barrier = pltpu.get_barrier_semaphore()
    for j in range(blocks):

        @pl.when(valid[j])
        def _():
            pl.semaphore_signal(barrier, inc=1, device_id=(peers[j],), device_id_type=MESH)

    for s in far:
        pl.semaphore_signal(barrier, inc=1, device_id=(partners[s],), device_id_type=MESH)

    for i in range(3):
        n2[i, 0:4, :] = nrm[i]
        n2[i, 4:8, :] = nrm[i]
    for eb in range(eb_count):
        lanes = slice(eb * LANES, (eb + 1) * LANES)
        spread = pl.ds(eb, 4, stride=eb_count)
        for i in range(3):
            nd[pl.ds(i * rows + eb, 4, stride=eb_count), :] = nrm[i, :, lanes]
        half_scale[spread, :] = 0.5 * fsc[:, lanes]
        code_d[spread, :] = nbr[:, lanes]
        orient_d[spread, :] = ori[:, lanes]
        mat_d[spread, :] = mat[:, lanes]

    def reflect_rows(g, carry):
        at = pl.ds(pl.multiple_of(g * SUB, SUB), SUB)
        kind = mat_d[at, :]
        picked = jnp.zeros((SUB, LANES), jnp.float32)
        for m in range(materials):
            picked = jnp.where(kind == m, imp[m], picked)
        reflect = (picked - 1.0) / (picked + 1.0)
        reflect_d[at, :] = reflect
        loss = 0.5 * half_scale[at, :] * (1.0 - reflect * reflect)
        loss_d[at, :] = jnp.where(code_d[at, :] < 0, loss, 0.0)
        return carry

    for field in range(4):
        nat[field * PAD + SLOT : (field + 1) * PAD, :] = jnp.zeros((PAD - SLOT, elems), jnp.float32)

    def copy_out(section, j):
        return pltpu.make_async_remote_copy(
            src_ref=send_buf.at[pl.ds((section * blocks + j) * SLOT, SLOT), :],
            dst_ref=recv_buf.at[pl.ds((section * blocks + blocks - 1 - j) * SLOT, SLOT), :],
            send_sem=send_sem.at[section, j],
            recv_sem=recv_sem.at[section, blocks - 1 - j],
            device_id=(peers[j],),
            device_id_type=MESH,
        )

    def copy_in(section, j):
        return pltpu.make_async_remote_copy(
            src_ref=send_buf.at[pl.ds((section * blocks + j) * SLOT, SLOT), :],
            dst_ref=recv_buf.at[pl.ds((section * blocks + j) * SLOT, SLOT), :],
            send_sem=send_sem.at[section, j],
            recv_sem=recv_sem.at[section, j],
            device_id=(peers[j],),
            device_id_type=MESH,
        )

    def hot_rows(codes, column):
        low = jnp.broadcast_to(codes & (LANES - 1), (LANES, LANES))
        one = jnp.where(lax.broadcasted_iota(jnp.int32, (LANES, LANES), 0) == low, 1.0, 0.0)
        one = one.astype(jnp.bfloat16)
        hot[0:LANES, pl.ds(column, LANES)] = one
        hot[LANES : 2 * LANES, pl.ds(column, LANES)] = one

    def hot_face_row(r, carry):
        hot_rows(code_d[pl.ds(r, 1), :], pl.multiple_of(r * LANES, LANES))
        return carry

    for j in range(blocks):
        hot_rows(snd[j : j + 1, :], (rows + j) * LANES)

    half = rows // 2

    def main_at(k):
        return (k // half) * half * 10 + (k % half) * SUB

    def rest_at(q):
        return (q // (groups // 2)) * half * 10 + half * SUB + (q % (groups // 2)) * SLOT

    def fill_table():
        for pair in range(half):
            value = jnp.concatenate(
                [tab[pl.ds(pair * 2 + h, SUB, stride=rows), :] for h in range(2)], axis=0
            )
            put_split(main_at(pair * 2), value)
        for q in range(groups):
            value = jnp.concatenate(
                [tab[n * rows + q * SUB : n * rows + (q + 1) * SUB, :] for n in (8, 9)], axis=0
            )
            put_split(rest_at(q), value)

    def spread_rows(g, carry):
        first = pl.multiple_of(g * SUB, SUB)
        value = tab[pl.ds(first, SUB), :]
        for r in range(SUB):
            spot = pl.multiple_of((first + r) * SUB, SUB)
            spread_tab[pl.ds(spot, SUB), :] = jnp.broadcast_to(value[r : r + 1], (SUB, LANES))
        return carry

    def pick_some(values, code, start, count):
        high = (code >> 7) - start
        low = code & (LANES - 1)
        values = list(values)
        for k in range(count):
            hit = high == k
            for n in range(10):
                spot = pl.multiple_of((n * rows + start + k) * SUB, SUB)
                source = spread_tab[pl.ds(spot, SUB), :]
                values[n] = jnp.where(hit, lane_pick(source, low), values[n])
        return values

    def put_split(first, value):
        high = value.astype(jnp.bfloat16)
        table[first : first + SLOT, 0:LANES] = high
        table[first : first + SLOT, LANES : 2 * LANES] = (
            value - high.astype(jnp.float32)
        ).astype(jnp.bfloat16)

    def pick_tile(column, codes, halves):
        product = jnp.dot(
            table[0 : halves * half * 10, :],
            hot[:, pl.ds(column, 2 * LANES)],
            preferred_element_type=jnp.float32,
        )
        found = []
        for h in range(2):
            lanes = slice(h * LANES, (h + 1) * LANES)
            high = jnp.broadcast_to(codes[h] >> 7, (SUB, LANES))
            main = jnp.zeros((SUB, LANES), jnp.float32)
            for k in range(halves * half):
                main = jnp.where(high == k, product[main_at(k) : main_at(k) + SUB, lanes], main)
            within = high - lax.broadcasted_iota(jnp.int32, (SUB, LANES), 0)
            rest = [jnp.zeros((SUB, LANES), jnp.float32) for _ in range(2)]
            for q in range(halves * groups // 2):
                hit = within == q * SUB
                for r in range(2):
                    first = rest_at(q) + r * SUB
                    rest[r] = jnp.where(hit, product[first : first + SUB, lanes], rest[r])
            found.append((main, [jnp.sum(r, axis=0, keepdims=True) for r in rest]))
        return found

    def part_copy(s):
        return pltpu.make_async_remote_copy(
            src_ref=part_sent.at[s],
            dst_ref=part_got.at[s],
            send_sem=part_send_sem.at[s],
            recv_sem=part_recv_sem.at[s],
            device_id=(partners[s],),
            device_id_type=MESH,
        )

    def advance(s):
        if s >= stages:
            return
        part_copy(s).wait_recv()
        total = part_sent[s] + part_got[s]
        if s + 1 < stages:
            part_sent[s + 1] = total
            part_copy(s + 1).start()
            return
        ones = jnp.ones((SUB, LANES), jnp.float32)
        for section in range(2):
            sums = lax.dot_general(
                ones,
                total[section * materials : (section + 1) * materials],
                (((1,), (1,)), ((), ())),
                precision=lax.Precision.HIGHEST,
                preferred_element_type=jnp.float32,
            )
            tot_out[section : section + 1, :] = sums[0:1] * (NMAT / (devices * elems))

    for section in range(2):
        sol_in = sol if section == 0 else sol_out
        reg_in = reg if section == 0 else reg_out

        for node in range(20):
            for eb in range(eb_count):
                place = pl.ds(node * 4 * eb_count + eb, 4, stride=eb_count)
                xd[place, :] = sol_in[node, :, eb * LANES : (eb + 1) * LANES]

        for f in range(4):
            normal = [nd[i * rows + f * eb_count : i * rows + (f + 1) * eb_count, :] for i in range(3)]
            for n in range(10):
                node = face_nodes[f][n]
                press, u, v, w = [
                    xd[(node * 4 + field) * eb_count : (node * 4 + field + 1) * eb_count, :]
                    for field in range(4)
                ]
                un = normal[0] * u + normal[1] * v + normal[2] * w
                spot = slice(n * rows + f * eb_count, n * rows + (f + 1) * eb_count)
                tab[spot, :] = press + un
                hd[spot, :] = un - press

        fill_table()

        lax.fori_loop(0, 10 * groups, spread_rows, 0, unroll=4)

        picked = pick_some([jnp.zeros((SUB, LANES), jnp.float32)] * 10, snd[...], half, half)
        for first in range(0, blocks, 2):
            column = (rows + first) * LANES
            found = pick_tile(column, [snd[first + h : first + h + 1, :] for h in range(2)], 1)
            for h in range(2):
                at = (section * blocks + first + h) * SLOT
                main, rest = found[h]
                send_buf[at : at + SUB, :] = main
                for r in range(2):
                    send_buf[at + SUB + r : at + SUB + r + 1, :] = rest[r]
        for n in range(10):
            place = pl.ds(section * blocks * SLOT + n, blocks, stride=SLOT)
            send_buf[place, :] = send_buf[place, :] + picked[n]

        if section == 0:
            expected = len(far) + sum(v.astype(jnp.int32) for v in valid)
            pl.semaphore_wait(barrier, expected)
        for j in range(blocks):

            @pl.when(valid[j])
            def _():
                copy_out(section, j).start()

        if section == 0:
            lax.fori_loop(0, groups, reflect_rows, 0)
            lax.fori_loop(0, rows, hot_face_row, 0, unroll=2)

        def loss_rows(g, sums):
            at = pl.multiple_of(g * SUB, SUB)
            total = jnp.zeros((SUB, LANES), jnp.float32)
            for n in range(10):
                value = tab[pl.ds(pl.multiple_of(n * rows + at, SUB), SUB), :]
                total = total + value * value
            total = total * loss_d[pl.ds(at, SUB), :]
            kind = mat_d[pl.ds(at, SUB), :]
            return tuple(s + jnp.where(kind == m, total, 0.0) for m, s in enumerate(sums))

        sums = lax.fori_loop(
            0,
            groups,
            loss_rows,
            tuple(jnp.zeros((SUB, LANES), jnp.float32) for _ in range(materials)),
        )
        for m in range(materials):
            spot = section * materials + m
            part_sent[0, spot : spot + 1, :] = jnp.sum(sums[m], axis=0, keepdims=True)
        if section == 1:
            part_copy(0).start()

        for field in range(4):
            for first in range(0, 20, SUB):
                count = min(SUB, 20 - first)
                for eb in range(eb_count):
                    place = pl.ds((first * 4 + field) * eb_count + eb, count, stride=4 * eb_count)
                    spot = field * PAD + first
                    nat[spot : spot + count, eb * LANES : (eb + 1) * LANES] = xd[place, :]

        def volume_chunk(c):
            at = pl.ds(pl.multiple_of(c * CHUNK, CHUNK), CHUNK)
            press, u, v, w = [nat[f * PAD : (f + 1) * PAD, at] for f in range(4)]
            metric = [geo[i : i + 1, at] for i in range(9)]
            terms = [metric[a] * u + metric[3 + a] * v + metric[6 + a] * w for a in range(3)]
            terms = terms + [metric[i] * press for i in range(9)]
            vol[:, at] = split_dot(vol_parts[...], jnp.concatenate(terms, axis=0))

        def matmul_pair(q):
            first = q * 2
            column = pl.multiple_of(first * LANES, 2 * LANES)
            found = pick_tile(column, [code_d[pl.ds(first + h, 1), :] for h in range(2)], 2)
            for h in range(2):
                main, rest = found[h]
                acc[pl.ds(first + h, SUB, stride=rows), :] = main
                for r in range(2):
                    acc[pl.ds((SUB + r) * rows + first + h, 1), :] = rest[r]

        def pick_rows(at, start, count):
            at = pl.multiple_of(at, SUB)
            planes = [pl.ds(pl.multiple_of(n * rows + at, SUB), SUB) for n in range(10)]
            values = [acc[plane, :] for plane in planes]
            values = pick_some(values, code_d[pl.ds(at, SUB), :], start, count)
            for n in range(10):
                acc[planes[n], :] = values[n]

        def local_step(i, carry):
            volume_chunk(i)
            matmul_pair(2 * i)
            matmul_pair(2 * i + 1)
            pick_rows(half + (i // 2) * SUB, (i % 2) * half, half)
            return carry

        for n in range(10):
            acc[n * rows + half : (n + 1) * rows, :] = jnp.zeros((half, LANES), jnp.float32)
        if section == 0:
            lax.fori_loop(0, groups, local_step, 0)
        else:
            lax.fori_loop(0, groups // 2, local_step, 0)
            advance(0)
            lax.fori_loop(groups // 2, groups, local_step, 0)
            advance(1)

        for j in range(blocks):

            @pl.when(valid[j])
            def _():
                copy_in(section, j).wait_recv()

        for j in range(blocks):
            for n in range(10):
                spot = (section * blocks + j) * SLOT + n
                to = (j * 10 + n) * SUB
                spread_recv[to : to + SUB, :] = jnp.broadcast_to(
                    recv_buf[spot : spot + 1, :], (SUB, LANES)
                )

        def finish_rows(g, carry):
            at = pl.multiple_of(g * SUB, SUB)
            here = pl.ds(at, SUB)
            code = code_d[here, :]
            high = code >> 7
            low = code & (LANES - 1)
            planes = [pl.ds(pl.multiple_of(n * rows + at, SUB), SUB) for n in range(10)]
            values = [acc[planes[n], :] for n in range(10)]
            for j in range(blocks):
                hit = high == rows + j
                for n in range(10):
                    spot = (j * 10 + n) * SUB
                    source = spread_recv[spot : spot + SUB, :]
                    values[n] = jnp.where(hit, lane_pick(source, low), values[n])
            turn = orient_d[here, :]
            wall = code < 0
            reflect = reflect_d[here, :]
            scale = half_scale[here, :]
            for n in range(10):
                seen = jnp.where(
                    turn == 0,
                    values[rotations[0][n]],
                    jnp.where(turn == 1, values[rotations[1][n]], values[rotations[2][n]]),
                )
                seen = jnp.where(wall, reflect * tab[planes[n], :], seen)
                hd[planes[n], :] = scale * (hd[planes[n], :] + seen)
            return carry

        lax.fori_loop(0, groups, finish_rows, 0)
        if section == 1:
            advance(2)

        for eb in range(eb_count):
            lanes = slice(eb * LANES, (eb + 1) * LANES)
            normal = [n2[i, :, lanes] for i in range(3)]
            for kb in range(5):
                flux = hd[pl.ds(kb * SUB * eb_count + eb, SUB, stride=eb_count), :]
                fl[kb * SUB : (kb + 1) * SUB, lanes] = flux
                for i in range(3):
                    first = 40 * (i + 1) + kb * SUB
                    fl[first : first + SUB, lanes] = -normal[i] * flux

        if section == 1:
            advance(3)

        def update_chunk(c, carry):
            at = pl.ds(pl.multiple_of(c * CHUNK, CHUNK), CHUNK)
            rhs = split_dot(lift_parts[...], fl[:, at]) + vol[:, at]
            for node in range(20):
                change = time_step * rhs[node * 4 : node * 4 + 4]
                new = section_decay[section] * reg_in[node, :, at] + change
                sol_out[node, :, at] = sol_in[node, :, at] + section_weight[section] * new
                reg_out[node, :, at] = new
            return carry

        lax.fori_loop(0, elems // CHUNK, update_chunk, 0, unroll=4)

    for s in range(4, stages):
        advance(s)
    for s in range(stages):
        part_copy(s).wait_send()

    for section in range(2):
        for j in range(blocks):

            @pl.when(valid[j])
            def _():
                copy_out(section, j).wait_send()


def local(
    solution,
    register,
    geometry,
    normals,
    face_scale,
    impedance,
    neighbour,
    orientation,
    wall_material,
    send_faces,
):
    volume, lift, face_nodes, rotations = operator_tables()
    tables = (split_table(volume), split_table(lift))
    elems = solution.shape[2]
    rows = 4 * elems // LANES
    blocks = send_faces.shape[0]
    materials = impedance.shape[0]
    devices = lax.axis_size("dom")
    stages = devices.bit_length() - 1
    f32, i32 = (jnp.float32, jnp.int32)
    vmem = pl.BlockSpec(memory_space=pltpu.VMEM)
    smem = pl.BlockSpec(memory_space=pltpu.SMEM)
    out, register_out, absorbed = pl.pallas_call(
        functools.partial(step_kernel, devices, face_nodes, rotations),
        out_shape=(
            jax.ShapeDtypeStruct((20, 4, elems), f32),
            jax.ShapeDtypeStruct((20, 4, elems), f32),
            jax.ShapeDtypeStruct((2, materials), f32),
        ),
        in_specs=[vmem] * 5 + [smem] + [vmem] * 6,
        out_specs=(vmem, vmem, vmem),
        scratch_shapes=[
            pltpu.VMEM((20 * rows, LANES), f32),
            pltpu.VMEM((10 * rows, LANES), f32),
            pltpu.VMEM((10 * rows, LANES), f32),
            pltpu.VMEM((10 * rows, LANES), f32),
            pltpu.VMEM((3 * rows, LANES), f32),
            pltpu.VMEM((3, SUB, elems), f32),
            pltpu.VMEM((rows, LANES), i32),
            pltpu.VMEM((rows, LANES), i32),
            pltpu.VMEM((rows, LANES), i32),
            pltpu.VMEM((rows, LANES), f32),
            pltpu.VMEM((rows, LANES), f32),
            pltpu.VMEM((rows, LANES), f32),
            pltpu.VMEM((4 * PAD, elems), f32),
            pltpu.VMEM((80, elems), f32),
            pltpu.VMEM((160, elems), f32),
            pltpu.VMEM((2 * blocks * SLOT, LANES), f32),
            pltpu.VMEM((2 * blocks * SLOT, LANES), f32),
            pltpu.VMEM((2 * LANES, (rows + blocks) * LANES), jnp.bfloat16),
            pltpu.VMEM((10 * rows, 2 * LANES), jnp.bfloat16),
            pltpu.VMEM((10 * rows * SUB, LANES), f32),
            pltpu.VMEM((10 * blocks * SUB, LANES), f32),
            pltpu.VMEM((stages, 2 * materials, LANES), f32),
            pltpu.VMEM((stages, 2 * materials, LANES), f32),
            pltpu.SemaphoreType.DMA((2, blocks)),
            pltpu.SemaphoreType.DMA((2, blocks)),
            pltpu.SemaphoreType.DMA((stages,)),
            pltpu.SemaphoreType.DMA((stages,)),
        ],
        compiler_params=pltpu.CompilerParams(
            collective_id=0, has_side_effects=True, vmem_limit_bytes=40 * 1024 * 1024
        ),
    )(
        jnp.transpose(solution, (1, 0, 2)),
        jnp.transpose(register, (1, 0, 2)),
        geometry,
        normals,
        face_scale,
        impedance,
        neighbour,
        orientation,
        wall_material,
        send_faces,
        *tables,
    )
    out = jnp.transpose(out, (1, 0, 2))
    register_out = jnp.transpose(register_out, (1, 0, 2))
    return (out, register_out, absorbed)


def solution(mesh):
    in_specs = (
        P(None, None, "dom"),
        P(None, None, "dom"),
        P(None, "dom"),
        P(None, None, "dom"),
        P(None, "dom"),
        P(),
        P(None, "dom"),
        P(None, "dom"),
        P(None, "dom"),
        P("dom", None),
    )
    out_specs = (P(None, None, "dom"), P(None, None, "dom"), P())
    return jax.shard_map(local, mesh=mesh, in_specs=in_specs, out_specs=out_specs, check_vma=False)
```

```python
import functools
import math

import jax
import jax.numpy as jnp
import numpy as np
from jax import lax
from jax.experimental import pallas as pl
from jax.experimental.pallas import tpu as pltpu
from jax.sharding import PartitionSpec as P

NMAT = 16


section_decay = (-567301805773.0 / 1357537059087.0, -2404267990393.0 / 2016746695238.0)
section_weight = (1720146321549.0 / 2090206949498.0, 3134564353537.0 / 4481467310338.0)
time_step = 0.002


def mat_product(left, right):
    inner = len(right)
    return [
        [sum((left[i][k] * right[k][j] for k in range(inner))) for j in range(len(right[0]))]
        for i in range(len(left))
    ]


def flipped(matrix):
    return [list(row) for row in zip(*matrix)]


def solve_rows(matrix, right):
    size = len(matrix)
    augmented = [list(matrix[i]) + list(right[i]) for i in range(size)]
    for column in range(size):
        pivot = max(range(column, size), key=lambda r: abs(augmented[r][column]))
        augmented[column], augmented[pivot] = (augmented[pivot], augmented[column])
        leader = augmented[column][column]
        augmented[column] = [value / leader for value in augmented[column]]
        for other in range(size):
            if other != column:
                factor = augmented[other][column]
                if factor != 0.0:
                    augmented[other] = [
                        a - factor * b for a, b in zip(augmented[other], augmented[column])
                    ]
    return [row[size:] for row in augmented]


def identity_rows(size):
    return [[1.0 if i == j else 0.0 for j in range(size)] for i in range(size)]


def dg_tables():
    lattice = [(i, j, k) for i in range(4) for j in range(4 - i) for k in range(4 - i - j)]
    coords = [(i / 3.0, j / 3.0, k / 3.0) for i, j, k in lattice]
    vander = [[x**a * y**b * z**c for a, b, c in lattice] for x, y, z in coords]
    inverse = solve_rows(vander, identity_rows(20))
    gradient_rows = []
    for d in range(3):
        derived = []
        for point in coords:
            row = []
            for powers in lattice:
                if powers[d] == 0:
                    row.append(0.0)
                else:
                    lowered = [powers[0], powers[1], powers[2]]
                    lowered[d] = lowered[d] - 1
                    row.append(
                        powers[d]
                        * point[0] ** lowered[0]
                        * point[1] ** lowered[1]
                        * point[2] ** lowered[2]
                    )
            derived.append(row)
        gradient_rows.extend(mat_product(derived, inverse))
    mono_mass = [
        [
            math.factorial(a + p)
            * math.factorial(b + q)
            * math.factorial(c + r)
            / math.factorial(a + b + c + p + q + r + 3)
            for p, q, r in lattice
        ]
        for a, b, c in lattice
    ]
    mass_matrix = mat_product(mat_product(flipped(inverse), mono_mass), inverse)
    plane_points = [(a, b) for a in range(4) for b in range(4 - a)]
    face_coords = [(a / 3.0, b / 3.0) for a, b in plane_points]
    vander_face = [[x**a * y**b for a, b in plane_points] for x, y in face_coords]
    inverse_face = solve_rows(vander_face, identity_rows(10))
    mono_face = [
        [
            math.factorial(a + p) * math.factorial(b + q) / math.factorial(a + b + p + q + 2)
            for p, q in plane_points
        ]
        for a, b in plane_points
    ]
    face_mass = mat_product(mat_product(flipped(inverse_face), mono_face), inverse_face)
    position = {point: n for n, point in enumerate(lattice)}
    builders = [
        lambda a, b: (a, b, 0),
        lambda a, b: (a, 0, b),
        lambda a, b: (0, a, b),
        lambda a, b: (a, b, 3 - a - b),
    ]
    face_nodes = [[position[builder(a, b)] for a, b in plane_points] for builder in builders]
    surface = [[0.0] * 40 for n in range(20)]
    for f in range(4):
        for n in range(10):
            for m in range(10):
                surface[face_nodes[f][n]][f * 10 + m] = face_mass[n][m]
    lift_matrix = solve_rows(mass_matrix, surface)
    rotations = []
    for t in range(3):
        mapping = []
        for a, b in plane_points:
            triple = (b, a, 3 - a - b)
            for s in range(t):
                triple = (triple[1], triple[2], triple[0])
            mapping.append(plane_points.index((triple[0], triple[1])))
        rotations.append(mapping)
    return (gradient_rows, lift_matrix, face_nodes, rotations)


def peer_offsets(half_span):
    return [j - half_span if j < half_span else j - half_span + 1 for j in range(2 * half_span)]


LANES = 128
SUB = 8
PAD = 24
SLOT = 16
CHUNK = 256
MESH = pl.DeviceIdType.MESH


def operator_tables():
    grad_rows, lift_rows, face_nodes, rotations = dg_tables()
    grads = np.array(grad_rows, dtype=np.float64).reshape(3, 20, 20)
    volume = np.zeros((80, 12 * PAD))
    for a in range(3):
        volume[0::4, a * PAD : a * PAD + 20] = -grads[a]
        for i in range(3):
            first = (3 + 3 * i + a) * PAD
            volume[i + 1 :: 4, first : first + 20] = -grads[a]
    lift_node_major = np.array(
        [[row[f * 10 + m] for m in range(10) for f in range(4)] for row in lift_rows]
    )
    lift = np.zeros((80, 160))
    for field in range(4):
        lift[field::4, field * 40 : field * 40 + 40] = lift_node_major
    return (volume, lift, face_nodes, rotations)


def split_table(table):
    single = jnp.asarray(table, dtype=jnp.float32)
    high = single.astype(jnp.bfloat16)
    low = (single - high.astype(jnp.float32)).astype(jnp.bfloat16)
    return jnp.concatenate([high, high, low], axis=1)


def split_dot(parts, values):
    high = values.astype(jnp.bfloat16)
    low = (values - high.astype(jnp.float32)).astype(jnp.bfloat16)
    stacked = jnp.concatenate([high, low, high], axis=0)
    return jnp.dot(parts, stacked, preferred_element_type=jnp.float32)


def lane_pick(row, lanes):
    source = jnp.broadcast_to(row, lanes.shape)
    return jnp.take_along_axis(source, lanes, axis=1, mode="promise_in_bounds")


def step_kernel(
    devices,
    face_nodes,
    rotations,
    *refs,
):
    inputs = refs[:12]
    (
        sol_out,
        reg_out,
        tot_out,
        xd,
        tab,
        hd,
        acc,
        nd,
        n2,
        code_d,
        orient_d,
        mat_d,
        half_scale,
        reflect_d,
        loss_d,
        nat,
        vol,
        fl,
        send_buf,
        recv_buf,
        hot,
        table,
        part_sent,
        part_got,
        send_sem,
        recv_sem,
        part_send_sem,
        part_recv_sem,
        in_sem,
        *held,
    ) = refs[12:]
    loads = [
        pltpu.make_async_copy(source, target, in_sem.at[i])
        for i, (source, target) in enumerate(zip(inputs, held))
    ]
    for i in (0, 3, 9, 2, 4, 5, 6, 7, 8, 10, 11, 1):
        loads[i].start()
    sol, reg, geo, nrm, fsc, imp, nbr, ori, mat, snd, vol_parts, lift_parts = held
    elems = sol.shape[2]
    eb_count = elems // LANES
    rows = 4 * eb_count
    groups = rows // SUB
    blocks = snd.shape[0]
    materials = imp.shape[0]
    offsets = peer_offsets(blocks // 2)
    me = lax.axis_index("dom")
    peers = [me + o for o in offsets]
    valid = [(p >= 0) & (p < devices) for p in peers]
    stages = devices.bit_length() - 1
    assert devices == 1 << stages
    partners = [me + (1 << s) - (2 << s) * ((me // (1 << s)) % 2) for s in range(stages)]
    far = [s for s in range(stages) if 1 << s > blocks // 2]

    recv_buf[...] = jnp.zeros_like(recv_buf)
    send_buf[...] = jnp.zeros_like(send_buf)
    barrier = pltpu.get_barrier_semaphore()
    for j in range(blocks):

        @pl.when(valid[j])
        def _():
            pl.semaphore_signal(barrier, inc=1, device_id=(peers[j],), device_id_type=MESH)

    for s in far:
        pl.semaphore_signal(barrier, inc=1, device_id=(partners[s],), device_id_type=MESH)

    loads[3].wait()
    for eb in range(eb_count):
        lanes = slice(eb * LANES, (eb + 1) * LANES)
        for i in range(3):
            nd[pl.ds(i * rows + eb, 4, stride=eb_count), :] = nrm[i, :, lanes]

    def face_tables():
        for i in (4, 5, 6, 7, 8):
            loads[i].wait()
        for i in range(3):
            n2[i, 0:4, :] = nrm[i]
            n2[i, 4:8, :] = nrm[i]
        for eb in range(eb_count):
            lanes = slice(eb * LANES, (eb + 1) * LANES)
            spread = pl.ds(eb, 4, stride=eb_count)
            half_scale[spread, :] = 0.5 * fsc[:, lanes]
            code_d[spread, :] = nbr[:, lanes]
            orient_d[spread, :] = ori[:, lanes]
            mat_d[spread, :] = mat[:, lanes]

    def reflect_rows(g, carry):
        at = pl.ds(pl.multiple_of(g * SUB, SUB), SUB)
        kind = mat_d[at, :]
        picked = jnp.zeros((SUB, LANES), jnp.float32)
        for m in range(materials):
            picked = jnp.where(kind == m, imp[m], picked)
        reflect = (picked - 1.0) / (picked + 1.0)
        reflect_d[at, :] = reflect
        loss = 0.5 * half_scale[at, :] * (1.0 - reflect * reflect)
        loss_d[at, :] = jnp.where(code_d[at, :] < 0, loss, 0.0)
        return carry

    for field in range(4):
        nat[field * PAD + SLOT : (field + 1) * PAD, :] = jnp.zeros((PAD - SLOT, elems), jnp.float32)

    def copy_out(section, j):
        return pltpu.make_async_remote_copy(
            src_ref=send_buf.at[pl.ds((section * blocks + j) * SLOT, SLOT), :],
            dst_ref=recv_buf.at[pl.ds((section * blocks + blocks - 1 - j) * SLOT, SLOT), :],
            send_sem=send_sem.at[section, j],
            recv_sem=recv_sem.at[section, blocks - 1 - j],
            device_id=(peers[j],),
            device_id_type=MESH,
        )

    def copy_in(section, j):
        return pltpu.make_async_remote_copy(
            src_ref=send_buf.at[pl.ds((section * blocks + j) * SLOT, SLOT), :],
            dst_ref=recv_buf.at[pl.ds((section * blocks + j) * SLOT, SLOT), :],
            send_sem=send_sem.at[section, j],
            recv_sem=recv_sem.at[section, j],
            device_id=(peers[j],),
            device_id_type=MESH,
        )

    def hot_rows(codes, column):
        low = jnp.broadcast_to(codes & (LANES - 1), (LANES, LANES))
        one = jnp.where(lax.broadcasted_iota(jnp.int32, (LANES, LANES), 0) == low, 1.0, 0.0)
        one = one.astype(jnp.bfloat16)
        hot[0:LANES, pl.ds(column, LANES)] = one
        hot[LANES : 2 * LANES, pl.ds(column, LANES)] = one

    def hot_face_row(r, carry):
        hot_rows(code_d[pl.ds(r, 1), :], pl.multiple_of(r * LANES, LANES))
        return carry

    loads[9].wait()
    for j in range(blocks):
        hot_rows(snd[j : j + 1, :], (rows + j) * LANES)
    loads[0].wait()

    half = rows // 2

    def main_at(k):
        return (k // half) * half * 10 + (k % half) * SUB

    def rest_at(q):
        return (q // (groups // 2)) * half * 10 + half * SUB + (q % (groups // 2)) * SLOT

    def fill_table():
        for pair in range(half):
            value = jnp.concatenate(
                [tab[pl.ds(pair * 2 + h, SUB, stride=rows), :] for h in range(2)], axis=0
            )
            put_split(main_at(pair * 2), value)
        for q in range(groups):
            value = jnp.concatenate(
                [tab[n * rows + q * SUB : n * rows + (q + 1) * SUB, :] for n in (8, 9)], axis=0
            )
            put_split(rest_at(q), value)

    def pick_some(values, code, start, count):
        high = (code >> 7) - start
        low = code & (LANES - 1)
        values = list(values)
        for k in range(count):
            hit = high == k
            for n in range(10):
                row = tab[pl.ds(n * rows + start + k, 1), :]
                values[n] = jnp.where(hit, lane_pick(row, low), values[n])
        return values

    def put_split(first, value):
        high = value.astype(jnp.bfloat16)
        table[first : first + SLOT, 0:LANES] = high
        table[first : first + SLOT, LANES : 2 * LANES] = (
            value - high.astype(jnp.float32)
        ).astype(jnp.bfloat16)

    def pick_tile(column, codes, halves):
        product = jnp.dot(
            table[0 : halves * half * 10, :],
            hot[:, pl.ds(column, 2 * LANES)],
            preferred_element_type=jnp.float32,
        )
        found = []
        for h in range(2):
            lanes = slice(h * LANES, (h + 1) * LANES)
            high = jnp.broadcast_to(codes[h] >> 7, (SUB, LANES))
            main = jnp.zeros((SUB, LANES), jnp.float32)
            for k in range(halves * half):
                main = jnp.where(high == k, product[main_at(k) : main_at(k) + SUB, lanes], main)
            within = high - lax.broadcasted_iota(jnp.int32, (SUB, LANES), 0)
            rest = [jnp.zeros((SUB, LANES), jnp.float32) for _ in range(2)]
            for q in range(halves * groups // 2):
                hit = within == q * SUB
                for r in range(2):
                    first = rest_at(q) + r * SUB
                    rest[r] = jnp.where(hit, product[first : first + SUB, lanes], rest[r])
            found.append((main, [jnp.sum(r, axis=0, keepdims=True) for r in rest]))
        return found

    def part_copy(s):
        return pltpu.make_async_remote_copy(
            src_ref=part_sent.at[s],
            dst_ref=part_got.at[s],
            send_sem=part_send_sem.at[s],
            recv_sem=part_recv_sem.at[s],
            device_id=(partners[s],),
            device_id_type=MESH,
        )

    def advance(s):
        if s >= stages:
            return
        part_copy(s).wait_recv()
        total = part_sent[s] + part_got[s]
        if s + 1 < stages:
            part_sent[s + 1] = total
            part_copy(s + 1).start()
            return
        ones = jnp.ones((SUB, LANES), jnp.float32)
        for section in range(2):
            sums = lax.dot_general(
                ones,
                total[section * materials : (section + 1) * materials],
                (((1,), (1,)), ((), ())),
                precision=lax.Precision.HIGHEST,
                preferred_element_type=jnp.float32,
            )
            tot_out[section : section + 1, :] = sums[0:1] * (NMAT / (devices * elems))

    for section in range(2):
        sol_in = sol if section == 0 else sol_out
        reg_in = reg if section == 0 else reg_out

        for node in range(20):
            for eb in range(eb_count):
                place = pl.ds(node * 4 * eb_count + eb, 4, stride=eb_count)
                xd[place, :] = sol_in[node, :, eb * LANES : (eb + 1) * LANES]

        for f in range(4):
            normal = [nd[i * rows + f * eb_count : i * rows + (f + 1) * eb_count, :] for i in range(3)]
            for n in range(10):
                node = face_nodes[f][n]
                press, u, v, w = [
                    xd[(node * 4 + field) * eb_count : (node * 4 + field + 1) * eb_count, :]
                    for field in range(4)
                ]
                un = normal[0] * u + normal[1] * v + normal[2] * w
                spot = slice(n * rows + f * eb_count, n * rows + (f + 1) * eb_count)
                tab[spot, :] = press + un
                hd[spot, :] = un - press

        fill_table()

        picked = pick_some([jnp.zeros((SUB, LANES), jnp.float32)] * 10, snd[...], half, half)
        for first in range(0, blocks, 2):
            column = (rows + first) * LANES
            found = pick_tile(column, [snd[first + h : first + h + 1, :] for h in range(2)], 1)
            for h in range(2):
                at = (section * blocks + first + h) * SLOT
                main, rest = found[h]
                send_buf[at : at + SUB, :] = main
                for r in range(2):
                    send_buf[at + SUB + r : at + SUB + r + 1, :] = rest[r]
        for n in range(10):
            place = pl.ds(section * blocks * SLOT + n, blocks, stride=SLOT)
            send_buf[place, :] = send_buf[place, :] + picked[n]

        if section == 0:
            expected = len(far) + sum(v.astype(jnp.int32) for v in valid)
            pl.semaphore_wait(barrier, expected)
        for j in range(blocks):

            @pl.when(valid[j])
            def _():
                copy_out(section, j).start()

        if section == 0:
            face_tables()
            lax.fori_loop(0, groups, reflect_rows, 0)
            lax.fori_loop(0, rows, hot_face_row, 0, unroll=2)

        def loss_rows(g, sums):
            at = pl.multiple_of(g * SUB, SUB)
            total = jnp.zeros((SUB, LANES), jnp.float32)
            for n in range(10):
                value = tab[pl.ds(pl.multiple_of(n * rows + at, SUB), SUB), :]
                total = total + value * value
            total = total * loss_d[pl.ds(at, SUB), :]
            kind = mat_d[pl.ds(at, SUB), :]
            return tuple(s + jnp.where(kind == m, total, 0.0) for m, s in enumerate(sums))

        sums = lax.fori_loop(
            0,
            groups,
            loss_rows,
            tuple(jnp.zeros((SUB, LANES), jnp.float32) for _ in range(materials)),
        )
        for m in range(materials):
            spot = section * materials + m
            part_sent[0, spot : spot + 1, :] = jnp.sum(sums[m], axis=0, keepdims=True)
        if section == 1:
            part_copy(0).start()

        for field in range(4):
            for first in range(0, 20, SUB):
                count = min(SUB, 20 - first)
                for eb in range(eb_count):
                    place = pl.ds((first * 4 + field) * eb_count + eb, count, stride=4 * eb_count)
                    spot = field * PAD + first
                    nat[spot : spot + count, eb * LANES : (eb + 1) * LANES] = xd[place, :]

        if section == 0:
            loads[2].wait()
            loads[10].wait()

        def volume_chunk(c):
            at = pl.ds(pl.multiple_of(c * CHUNK, CHUNK), CHUNK)
            press, u, v, w = [nat[f * PAD : (f + 1) * PAD, at] for f in range(4)]
            metric = [geo[i : i + 1, at] for i in range(9)]
            terms = [metric[a] * u + metric[3 + a] * v + metric[6 + a] * w for a in range(3)]
            terms = terms + [metric[i] * press for i in range(9)]
            vol[:, at] = split_dot(vol_parts[...], jnp.concatenate(terms, axis=0))

        def matmul_pair(q):
            first = q * 2
            column = pl.multiple_of(first * LANES, 2 * LANES)
            found = pick_tile(column, [code_d[pl.ds(first + h, 1), :] for h in range(2)], 2)
            for h in range(2):
                main, rest = found[h]
                acc[pl.ds(first + h, SUB, stride=rows), :] = main
                for r in range(2):
                    acc[pl.ds((SUB + r) * rows + first + h, 1), :] = rest[r]

        def pick_rows(at, start, count):
            at = pl.multiple_of(at, SUB)
            planes = [pl.ds(pl.multiple_of(n * rows + at, SUB), SUB) for n in range(10)]
            values = [acc[plane, :] for plane in planes]
            values = pick_some(values, code_d[pl.ds(at, SUB), :], start, count)
            for n in range(10):
                acc[planes[n], :] = values[n]

        def local_step(i, carry):
            volume_chunk(i)
            matmul_pair(2 * i)
            matmul_pair(2 * i + 1)
            pick_rows(half + (i // 2) * SUB, (i % 2) * half, half)
            return carry

        for n in range(10):
            acc[n * rows + half : (n + 1) * rows, :] = jnp.zeros((half, LANES), jnp.float32)
        if section == 0:
            lax.fori_loop(0, groups, local_step, 0)
        else:
            lax.fori_loop(0, groups // 2, local_step, 0)
            advance(0)
            lax.fori_loop(groups // 2, groups, local_step, 0)
            advance(1)

        for j in range(blocks):

            @pl.when(valid[j])
            def _():
                copy_in(section, j).wait_recv()

        def finish_rows(g, carry):
            at = pl.multiple_of(g * SUB, SUB)
            here = pl.ds(at, SUB)
            code = code_d[here, :]
            high = code >> 7
            low = code & (LANES - 1)
            planes = [pl.ds(pl.multiple_of(n * rows + at, SUB), SUB) for n in range(10)]
            values = [acc[planes[n], :] for n in range(10)]
            for j in range(blocks):
                hit = high == rows + j
                for n in range(10):
                    spot = (section * blocks + j) * SLOT + n
                    row = recv_buf[spot : spot + 1, :]
                    values[n] = jnp.where(hit, lane_pick(row, low), values[n])
            turn = orient_d[here, :]
            wall = code < 0
            reflect = reflect_d[here, :]
            scale = half_scale[here, :]
            for n in range(10):
                seen = jnp.where(
                    turn == 0,
                    values[rotations[0][n]],
                    jnp.where(turn == 1, values[rotations[1][n]], values[rotations[2][n]]),
                )
                seen = jnp.where(wall, reflect * tab[planes[n], :], seen)
                hd[planes[n], :] = scale * (hd[planes[n], :] + seen)
            return carry

        lax.fori_loop(0, groups, finish_rows, 0)
        if section == 1:
            advance(2)

        for eb in range(eb_count):
            lanes = slice(eb * LANES, (eb + 1) * LANES)
            normal = [n2[i, :, lanes] for i in range(3)]
            for kb in range(5):
                flux = hd[pl.ds(kb * SUB * eb_count + eb, SUB, stride=eb_count), :]
                fl[kb * SUB : (kb + 1) * SUB, lanes] = flux
                for i in range(3):
                    first = 40 * (i + 1) + kb * SUB
                    fl[first : first + SUB, lanes] = -normal[i] * flux

        if section == 1:
            advance(3)

        if section == 0:
            loads[11].wait()
            loads[1].wait()

        def update_chunk(c, carry):
            at = pl.ds(pl.multiple_of(c * CHUNK, CHUNK), CHUNK)
            rhs = split_dot(lift_parts[...], fl[:, at]) + vol[:, at]
            for node in range(20):
                change = time_step * rhs[node * 4 : node * 4 + 4]
                new = section_decay[section] * reg_in[node, :, at] + change
                sol_out[node, :, at] = sol_in[node, :, at] + section_weight[section] * new
                reg_out[node, :, at] = new
            return carry

        lax.fori_loop(0, elems // CHUNK, update_chunk, 0, unroll=4)

    for s in range(4, stages):
        advance(s)
    for s in range(stages):
        part_copy(s).wait_send()

    for section in range(2):
        for j in range(blocks):

            @pl.when(valid[j])
            def _():
                copy_out(section, j).wait_send()


def local(
    solution,
    register,
    geometry,
    normals,
    face_scale,
    impedance,
    neighbour,
    orientation,
    wall_material,
    send_faces,
):
    volume, lift, face_nodes, rotations = operator_tables()
    tables = (split_table(volume), split_table(lift))
    elems = solution.shape[2]
    rows = 4 * elems // LANES
    blocks = send_faces.shape[0]
    materials = impedance.shape[0]
    devices = lax.axis_size("dom")
    stages = devices.bit_length() - 1
    f32, i32 = (jnp.float32, jnp.int32)
    vmem = pl.BlockSpec(memory_space=pltpu.VMEM)
    arguments = (
        jnp.transpose(solution, (1, 0, 2)),
        jnp.transpose(register, (1, 0, 2)),
        geometry,
        normals,
        face_scale,
        impedance,
        neighbour,
        orientation,
        wall_material,
        send_faces,
        *tables,
    )
    held = [
        (pltpu.SMEM if a is impedance else pltpu.VMEM)(a.shape, a.dtype) for a in arguments
    ]
    hbm = pl.BlockSpec(memory_space=pltpu.HBM)
    out, register_out, absorbed = pl.pallas_call(
        functools.partial(step_kernel, devices, face_nodes, rotations),
        out_shape=(
            jax.ShapeDtypeStruct((20, 4, elems), f32),
            jax.ShapeDtypeStruct((20, 4, elems), f32),
            jax.ShapeDtypeStruct((2, materials), f32),
        ),
        in_specs=[hbm] * 12,
        out_specs=(vmem, vmem, vmem),
        scratch_shapes=[
            pltpu.VMEM((20 * rows, LANES), f32),
            pltpu.VMEM((10 * rows, LANES), f32),
            pltpu.VMEM((10 * rows, LANES), f32),
            pltpu.VMEM((10 * rows, LANES), f32),
            pltpu.VMEM((3 * rows, LANES), f32),
            pltpu.VMEM((3, SUB, elems), f32),
            pltpu.VMEM((rows, LANES), i32),
            pltpu.VMEM((rows, LANES), i32),
            pltpu.VMEM((rows, LANES), i32),
            pltpu.VMEM((rows, LANES), f32),
            pltpu.VMEM((rows, LANES), f32),
            pltpu.VMEM((rows, LANES), f32),
            pltpu.VMEM((4 * PAD, elems), f32),
            pltpu.VMEM((80, elems), f32),
            pltpu.VMEM((160, elems), f32),
            pltpu.VMEM((2 * blocks * SLOT, LANES), f32),
            pltpu.VMEM((2 * blocks * SLOT, LANES), f32),
            pltpu.VMEM((2 * LANES, (rows + blocks) * LANES), jnp.bfloat16),
            pltpu.VMEM((10 * rows, 2 * LANES), jnp.bfloat16),
            pltpu.VMEM((stages, 2 * materials, LANES), f32),
            pltpu.VMEM((stages, 2 * materials, LANES), f32),
            pltpu.SemaphoreType.DMA((2, blocks)),
            pltpu.SemaphoreType.DMA((2, blocks)),
            pltpu.SemaphoreType.DMA((stages,)),
            pltpu.SemaphoreType.DMA((stages,)),
            pltpu.SemaphoreType.DMA((12,)),
            *held,
        ],
        compiler_params=pltpu.CompilerParams(
            collective_id=0, has_side_effects=True, vmem_limit_bytes=63 * 1024 * 1024
        ),
    )(*arguments)
    out = jnp.transpose(out, (1, 0, 2))
    register_out = jnp.transpose(register_out, (1, 0, 2))
    return (out, register_out, absorbed)


def solution(mesh):
    in_specs = (
        P(None, None, "dom"),
        P(None, None, "dom"),
        P(None, "dom"),
        P(None, None, "dom"),
        P(None, "dom"),
        P(),
        P(None, "dom"),
        P(None, "dom"),
        P(None, "dom"),
        P("dom", None),
    )
    out_specs = (P(None, None, "dom"), P(None, None, "dom"), P())
    return jax.shard_map(local, mesh=mesh, in_specs=in_specs, out_specs=out_specs, check_vma=False)
```
